256 devices in a mesh: grp: 32 (over z_hi, y, core), sp: 8 (over z_lo, x).
Axes of the slice: x: 4, y: 4, z: 8 (z_hi: 4, z_lo: 2; z = z_hi * 2 + z_lo), core: 2. Of those that a mesh axis runs over, the one named last changes fastest.
Arguments:
- queries: bfloat16 [32768, 2048], P(('grp', 'sp')), may hold values from -6 to 6
- keys: bfloat16 [32768, 256], P(('grp', 'sp')), may hold values from -32 to 32
- values: bfloat16 [32768, 256], P(('grp', 'sp')), may hold values from -6 to 6
- grad_out: bfloat16 [32768, 2048], P(('grp', 'sp')), may hold values from -6 to 6
- group_of_row: int32 [32768, 1], P(('grp', 'sp')), may hold values from 0 to 31; in each aligned block of 128 rows (0 to 127, 128 to 255, ...) at most 8 rows name the same one
- head_slot: int32 [16], replicated, may hold values from 0 to 15, each once
Outputs:
- grad_queries: bfloat16 [32768, 2048], P(('grp', 'sp'))
- grad_keys: bfloat16 [32768, 256], P(('grp', 'sp'))
- grad_values: bfloat16 [32768, 256], P(('grp', 'sp'))
The draws below stay inside these ranges and needn't reach their ends.
Inputs may be any that keep to these rules, and one draw needn't show every extreme that they name: `group_of_row`: among the 128 rows of one device no plan group is named more than 8 times; on some device some group is named exactly 8 times. `head_slot`: each slot number appears once.
All inputs are finite; a program needn't handle non-finite values.
Results may differ from the reference program's by a relative error of at most 0.035.
Values may be sent and summed in bfloat16 or wider, within the bound.
No kernel may reach another device: no remote copies, remote signals or barrier semaphores. Data moves between devices by JAX's collectives and lax.ppermute only.
A program may use at most 64 MiB of HBM per device.

```python
import math
import jax
import jax.numpy as jnp
import numpy as np
from jax import lax

HD = 128
QH = 16
KVH = 2
GROUP_HEADS = 7
TOK_DEV = 128
CAP = 8
TOKENS = 32768
N_GRP = 32
N_SP = 8


def draw_queries(key, part):
    key = jax.random.fold_in(key, 3)
    normal_key = jax.random.fold_in(key, 0)
    result = jax.random.truncated_normal(normal_key, -6.0, 6.0, (TOKENS, QH * HD), jnp.float32)
    return result.astype(jnp.bfloat16)


def draw_keys(key, part):
    key = jax.random.fold_in(key, 5)
    result = jax.random.truncated_normal(key, -6.0, 6.0, (TOKENS, KVH * HD), jnp.float32)
    return result.astype(jnp.bfloat16)


def levels(rng, dims, cuts, low, high):
    gain = 1.0
    for axis_at, blocks in cuts:
        heights = jax.random.uniform(jax.random.fold_in(jax.random.fold_in(rng, 6), axis_at), (blocks,), jnp.float32, low / len(cuts), high / len(cuts))
        gain = gain * jnp.repeat(jnp.exp(heights), dims[axis_at] // blocks).reshape((-1,) + (1,) * (len(dims) - 1 - axis_at))
    return gain


def deal_out(own_key, own, number, rows, amount, top, most, lean):
    ranking = jax.random.permutation(own_key, amount)
    packed, common = portions_of(amount, rows * top, most, lean, True), portions_of(amount, rows * top, most, lean, False)
    places = jnp.arange(amount)

    def named(tallies, rotation):
        used = int((tallies > 0).sum())
        fixed = max(1, used // 4)
        moved = fixed + (places - fixed + rotation * (used - fixed)) % max(1, amount - fixed)
        return jnp.zeros((amount,), jnp.int32).at[ranking[jnp.where(places < fixed, places, moved)]].set(jnp.asarray(tallies, jnp.int32))

    tallies = jnp.where(number % 4 == 0, named(packed, number // 4), named(common, number - number // 4 - 1))
    mixed = jax.random.permutation(jax.random.fold_in(own, 3), amount)
    giver, taker = mixed[0:amount // 2 * 2:2], mixed[1:amount // 2 * 2:2]
    room = jnp.minimum(tallies[giver] - 1, most - tallies[taker]) // 2
    room = jnp.where((giver == ranking[0]) | (taker == ranking[0]) | (tallies[taker] == 0), 0, jnp.maximum(room, 0))
    moved = jax.random.randint(jax.random.fold_in(own, 4), (amount // 2,), 0, 1 << 20) % (room + 1)
    tallies = tallies.at[giver].add(-moved).at[taker].add(moved)
    items = jnp.searchsorted(jnp.cumsum(tallies), jnp.arange(rows * top), side="right").astype(jnp.int32)
    table = items.reshape(top, rows).T
    table = table[jax.random.permutation(jax.random.fold_in(own, 1), rows)]
    rotation = jax.random.randint(jax.random.fold_in(own, 2), (rows, 1), 0, top)
    return jnp.take_along_axis(table, (jnp.arange(top)[None, :] + rotation) % top, axis=1)


def portions_of(number_of, total, reach, lean, full):
    portions = [(1 << 20) // math.isqrt(rank ** lean) + 1 for rank in range(1, number_of + 1)]
    largest = reach if full else min(reach, max(-(-total // number_of), total * portions[0] // sum(portions)))
    least = 1 if total - largest >= number_of - 1 else 0
    given, spare = [largest] + [least] * (number_of - 1), total - largest - least * (number_of - 1)
    while spare > 0:
        movable = [i for i in range(1, number_of) if given[i] < largest] or [i for i in range(1, number_of) if given[i] < reach]
        pool, remaining = sum([portions[i] for i in movable]), spare
        for i in movable:
            extra = min(reach - given[i], max(1, remaining * portions[i] // pool), spare)
            given[i] = given[i] + extra
            spare = spare - extra
    return np.array(given)


def scatter_about(key, dims, deviation, most, cuts=(), kind=jnp.bfloat16):
    gain = levels(key, dims, cuts, -0.22, 0.18) if cuts else 1.0
    values = jax.random.normal(key, dims, jnp.float32) * deviation * gain
    return jnp.minimum(jnp.maximum(values, -most), most).astype(kind)


def setup_inputs(seed: int = 0) -> dict:
    arg_keys = jax.random.split(jax.random.key(seed), 7)
    queries = draw_queries(jax.random.fold_in(arg_keys[6], 71), 0)
    keys = draw_keys(jax.random.fold_in(arg_keys[6], 71), 0)
    values = scatter_about(arg_keys[2], (TOKENS, KVH * HD), 1.0, 6.0, ((0, 256),))
    grad_out = scatter_about(arg_keys[3], (TOKENS, QH * HD), 1.0, 6.0, ((0, 256),))
    group_of_row_keys = jax.random.split(jax.random.fold_in(arg_keys[4], 1), TOKENS // TOK_DEV)
    group_of_row_turns = jax.random.permutation(jax.random.fold_in(arg_keys[4], 3), TOKENS // TOK_DEV)
    group_of_row = jax.vmap(lambda own, number: deal_out(jax.random.fold_in(arg_keys[4], 2), own, number, TOK_DEV, N_GRP, 1, CAP, 2))(group_of_row_keys, group_of_row_turns).reshape((TOKENS, 1))
    head_slot = jax.random.permutation(arg_keys[5], QH).astype(jnp.int32)
    return dict(queries=queries, keys=keys, values=values, grad_out=grad_out, group_of_row=group_of_row, head_slot=head_slot)


def group_grads(query_part, grad_part, key_part, value_part, doc_ids, kv_weight, softmax_scale):
    query_wide = query_part.astype(jnp.float32)
    grad_wide = grad_part.astype(jnp.float32)
    key_slot = jnp.einsum("wcd,hc->whd", key_part.astype(jnp.float32), kv_weight)
    value_slot = jnp.einsum("wcd,hc->whd", value_part.astype(jnp.float32), kv_weight)
    scores = jnp.einsum("qhd,khd->hqk", query_wide, key_slot) * softmax_scale
    visible = doc_ids[:, None] == doc_ids[None, :]
    scores = jnp.where(visible[None], scores, -1e30)
    row_max = jnp.max(scores, axis=2, keepdims=True)
    shifted = jnp.exp(scores - row_max)
    attend = shifted / jnp.sum(shifted, axis=2, keepdims=True)
    grad_attend = jnp.einsum("qhd,khd->hqk", grad_wide, value_slot)
    row_dot = jnp.sum(attend * grad_attend, axis=2, keepdims=True)
    grad_score = lax.optimization_barrier((attend * (grad_attend - row_dot) * softmax_scale).astype(jnp.bfloat16))
    grad_score = grad_score.astype(jnp.float32)
    attend_half = lax.optimization_barrier(attend.astype(jnp.bfloat16)).astype(jnp.float32)
    grad_query = jnp.einsum("hqk,khd->qhd", grad_score, key_slot).astype(jnp.bfloat16)
    key_slots = jnp.einsum("hqk,qhd->khd", grad_score, query_wide)
    value_slots = jnp.einsum("hqk,qhd->khd", attend_half, grad_wide)
    grad_key = jnp.einsum("khd,hc->kcd", key_slots, kv_weight)
    grad_value = jnp.einsum("khd,hc->kcd", value_slots, kv_weight)
    return grad_query, grad_key, grad_value


def reference(queries, keys, values, grad_out, group_of_row, head_slot):
    tokens = queries.shape[0]
    group_width = 2 * TOK_DEV * N_SP
    softmax_scale = HD ** -0.5
    row_group = group_of_row[:, 0].astype(jnp.int32)
    real_slot = head_slot < GROUP_HEADS * KVH
    kv_slot = jnp.minimum(head_slot // GROUP_HEADS, KVH - 1).astype(jnp.int32)
    kv_weight = (kv_slot[:, None] == jnp.arange(KVH, dtype=jnp.int32)[None, :]).astype(jnp.float32)
    masked = grad_out.reshape(tokens, QH, HD) * real_slot.astype(jnp.bfloat16)[None, :, None]
    query_heads = queries.reshape(tokens, QH, HD)
    key_heads = keys.reshape(tokens, KVH, HD)
    value_heads = values.reshape(tokens, KVH, HD)
    sorted_rows = jnp.argsort(row_group, stable=True).astype(jnp.int32)
    member = (row_group[None, :] == jnp.arange(N_GRP, dtype=jnp.int32)[:, None]).astype(jnp.int32)
    counts = jnp.sum(member, axis=1).astype(jnp.int32)
    starts = (jnp.cumsum(counts) - counts).astype(jnp.int32)
    padded = jnp.concatenate([sorted_rows, jnp.zeros((group_width,), jnp.int32)])

    def one_group(group_index):
        members = lax.dynamic_slice(padded, (starts[group_index],), (group_width,))
        filled = jnp.arange(group_width, dtype=jnp.int32) < counts[group_index]
        doc_ids = jnp.where(filled, 0, -1).astype(jnp.int32)
        grad_query, grad_key, grad_value = group_grads(query_heads[members], masked[members], key_heads[members], value_heads[members], doc_ids, kv_weight, softmax_scale)
        return members, filled, grad_query, grad_key, grad_value

    members, filled, grad_query, grad_key, grad_value = lax.map(one_group, jnp.arange(N_GRP, dtype=jnp.int32))
    flat_rows = members.reshape(-1)
    flat_filled = filled.reshape(-1)

    def place(source, columns):
        row_values = jnp.where(flat_filled[:, None], source.reshape(N_GRP * group_width, columns).astype(jnp.float32), 0.0)
        return jnp.zeros((tokens, columns), jnp.float32).at[flat_rows].add(row_values)

    grad_queries = place(grad_query, QH * HD).astype(jnp.bfloat16)
    grad_keys = place(grad_key, KVH * HD).astype(jnp.bfloat16)
    grad_values = place(grad_value, KVH * HD).astype(jnp.bfloat16)
    return grad_queries, grad_keys, grad_values
```

```python
import math

import jax
import jax.numpy as jnp
from jax import lax
from jax.experimental import pallas as pl
from jax.experimental.pallas import tpu as pltpu
from jax.sharding import Mesh
from jax.sharding import PartitionSpec as P

HD = 128
QH = 16
KVH = 2
GROUP_HEADS = 7
CAP = 8
HALF = QH // KVH
EMPTY = 64.0
NEG = -1e30
AXES = ("zh", "y", "c", "zl", "x")
PLANE = ("y", "c", "x")
COLUMN = ("zh", "zl")
BF = jnp.bfloat16
F32 = jnp.float32
KEY_TILE = 256
VMEM = 56 * 1024 * 1024


def contract_last(left, right):
    return lax.dot_general(left, right, (((1,), (1,)), ((), ())), preferred_element_type=F32)


def dot(left, right):
    return jnp.dot(left, right, preferred_element_type=F32)


def row_slots(group_ref):
    rows = group_ref.shape[0]
    across = jnp.broadcast_to(group_ref[...].astype(F32), (rows, rows))
    along = across.T
    first = lax.broadcasted_iota(jnp.int32, (rows, rows), 0)
    second = lax.broadcasted_iota(jnp.int32, (rows, rows), 1)
    return across, along, across == along, first, second


def placer_of(group_ref, slots):
    rows = group_ref.shape[0]
    across, along, same, first, second = row_slots(group_ref)
    before = jnp.sum(jnp.where(same & (first < second), 1.0, 0.0), axis=0, keepdims=True)
    target = (along[:1] * CAP + before).astype(jnp.int32)
    return jnp.where(lax.broadcasted_iota(jnp.int32, (slots, rows), 0) == target, 1.0, 0.0).astype(BF)


def taker_of(group_ref, slots):
    rows = group_ref.shape[0]
    across, along, same, first, second = row_slots(group_ref)
    before = jnp.sum(jnp.where(same & (second < first), 1.0, 0.0), axis=1, keepdims=True)
    target = (across[:, :1] * CAP + before).astype(jnp.int32)
    return jnp.where(lax.broadcasted_iota(jnp.int32, (rows, slots), 1) == target, 1.0, 0.0).astype(BF)


def pack_kv_kernel(group_ref, key_ref, value_ref, out_ref):
    slots = out_ref.shape[0]
    placer = placer_of(group_ref, slots)
    filled = jnp.sum(placer.astype(F32), axis=1, keepdims=True)
    lane = lax.broadcasted_iota(jnp.int32, (slots, HD), 1)
    mark = jnp.where((lane == 0) & (filled < 0.5), EMPTY, 0.0)
    for c in range(KVH):
        cols = slice(c * HD, (c + 1) * HD)
        out_ref[:, 2 * c * HD : (2 * c + 1) * HD] = dot(placer, key_ref[:, cols]).astype(BF)
        out_ref[:, (2 * c + 1) * HD : (2 * c + 2) * HD] = (dot(placer, value_ref[:, cols]) + mark).astype(BF)


def pack_qg_kernel(order_ref, group_ref, query_ref, grad_ref, out_q_ref, out_g_ref, placer_ref):
    at = pl.program_id(0)

    @pl.when(at == 0)
    def _():
        placer_ref[...] = placer_of(group_ref, placer_ref.shape[0])

    placer = placer_ref[...]
    real = jnp.where(at % HALF < GROUP_HEADS, 1.0, 0.0)
    out_q_ref[...] = dot(placer, query_ref[...]).astype(BF)
    out_g_ref[...] = (dot(placer, grad_ref[...]) * real).astype(BF)


def attend_kernel(
    q_ref, g_ref, k_ref, v_ref, dkv_ref, dq_ref, s_ref, p_ref, dk_ref, dv_ref, bias_ref, kt_ref
):
    at = pl.program_id(0)
    keys = k_ref.shape[0]
    rows = q_ref.shape[0]
    tiles = keys // KEY_TILE
    scale = HD ** (-0.5)
    unit = scale * math.log2(math.e)

    @pl.when(at % HALF == 0)
    def _():
        dk_ref[...] = jnp.zeros_like(dk_ref)
        dv_ref[...] = jnp.zeros_like(dv_ref)
        empty = v_ref[:, :1].astype(F32) > 0.5 * EMPTY
        bias_ref[...] = jnp.broadcast_to(jnp.where(empty, NEG, 0.0), bias_ref.shape)
        kt_ref[...] = k_ref[...].T

    q = q_ref[...]
    g = g_ref[...]
    top = jnp.full((8, rows), -3e38, F32)
    for t in range(tiles):
        part = slice(t * KEY_TILE, (t + 1) * KEY_TILE)
        bias = bias_ref[part, :]
        s = contract_last(k_ref[part, :], q) + jnp.concatenate([bias] * (rows // HD), axis=1)
        s_ref[part, :] = s
        top = jnp.maximum(top, jnp.max(s.reshape(KEY_TILE // 8, 8, rows), axis=0))
    top = jnp.max(top, axis=0, keepdims=True)
    total = jnp.zeros((8, rows), F32)
    cross = jnp.zeros((8, rows), F32)
    for t in range(tiles):
        part = slice(t * KEY_TILE, (t + 1) * KEY_TILE)
        dp = contract_last(v_ref[part, :], g)
        e = jnp.exp2((s_ref[part, :] - top) * unit)
        s_ref[part, :] = e
        p_ref[part, :] = dp
        total = total + jnp.sum(e.reshape(KEY_TILE // 8, 8, rows), axis=0)
        cross = cross + jnp.sum((e * dp).reshape(KEY_TILE // 8, 8, rows), axis=0)
    share = 1.0 / jnp.sum(total, axis=0, keepdims=True)
    row_dot = jnp.sum(cross, axis=0, keepdims=True) * share
    dqt = jnp.zeros((HD, rows), F32)
    for t in range(tiles):
        part = slice(t * KEY_TILE, (t + 1) * KEY_TILE)
        p = s_ref[part, :] * share
        ds = (p * (p_ref[part, :] - row_dot)).astype(BF)
        dv_ref[part, :] += dot(p.astype(BF), g)
        dk_ref[part, :] += dot(ds, q)
        dqt += dot(kt_ref[:, part], ds)
    dq_ref[...] = (dqt * scale).T.astype(BF)

    @pl.when(at % HALF == HALF - 1)
    def _():
        dkv_ref[:, :HD] = (dk_ref[...] * scale).astype(BF)
        dkv_ref[:, HD:] = dv_ref[...].astype(BF)


def unpack_q_kernel(order_ref, group_ref, dq_ref, out_ref, taker_ref):
    @pl.when(pl.program_id(0) == 0)
    def _():
        taker_ref[...] = taker_of(group_ref, taker_ref.shape[1])

    out_ref[...] = dot(taker_ref[...], dq_ref[...]).astype(BF)


def unpack_kv_kernel(group_ref, dkv_ref, dk_ref, dv_ref):
    taker = taker_of(group_ref, dkv_ref.shape[0])
    for c in range(KVH):
        cols = slice(c * HD, (c + 1) * HD)
        dk_ref[:, cols] = dot(taker, dkv_ref[:, 2 * c * HD : (2 * c + 1) * HD]).astype(BF)
        dv_ref[:, cols] = dot(taker, dkv_ref[:, (2 * c + 1) * HD : (2 * c + 2) * HD]).astype(BF)


def struct(*shape):
    return jax.ShapeDtypeStruct(shape, BF)


def params():
    return pltpu.CompilerParams(vmem_limit_bytes=VMEM)


def per_device(queries, keys, values, grad_out, group_of_row, head_slot):
    rows = queries.shape[0]
    groups = lax.axis_size(PLANE)
    column = lax.axis_size(COLUMN)
    slots = groups * CAP
    width_q = QH * HD
    width_kv = 2 * KVH * HD
    all_keys = column * slots

    def over_plane(array):
        return lax.all_to_all(array, PLANE, split_axis=0, concat_axis=0, tiled=True)

    position = jnp.arange(QH, dtype=jnp.int32)
    head_at = jnp.where(
        position % HALF == GROUP_HEADS,
        KVH * GROUP_HEADS + position // HALF,
        position // HALF * GROUP_HEADS + position % HALF,
    )
    order = jnp.sum(
        jnp.where(head_at[:, None] == head_slot[None, :], position[None, :], 0), axis=1
    ).astype(jnp.int32)

    sent_kv = pl.pallas_call(
        pack_kv_kernel,
        out_shape=struct(slots, width_kv),
        compiler_params=params(),
        name="pack_kv",
    )(group_of_row, keys, values)
    home_kv = over_plane(sent_kv)
    all_kv = lax.all_gather(home_kv, COLUMN, axis=0, tiled=True)

    whole = pl.BlockSpec((rows, 1), lambda p, order: (0, 0))
    from_slot = pl.BlockSpec((rows, HD), lambda p, order: (0, order[p]))
    to_sorted = pl.BlockSpec((slots, HD), lambda p, order: (0, p))
    sent_q, sent_g = pl.pallas_call(
        pack_qg_kernel,
        out_shape=(struct(slots, width_q), struct(slots, width_q)),
        grid_spec=pltpu.PrefetchScalarGridSpec(
            num_scalar_prefetch=1,
            grid=(QH,),
            in_specs=[whole, from_slot, from_slot],
            out_specs=[to_sorted, to_sorted],
            scratch_shapes=[pltpu.VMEM((slots, rows), BF)],
        ),
        compiler_params=params(),
        name="pack_qg",
    )(order, group_of_row, queries, grad_out)
    home_q = over_plane(sent_q)
    home_g = over_plane(sent_g)

    one_head = pl.BlockSpec((slots, HD), lambda p: (0, p))
    pairs = QH * slots * all_keys
    grad_kv, grad_q = pl.pallas_call(
        attend_kernel,
        out_shape=(struct(all_keys, width_kv), struct(slots, width_q)),
        grid=(QH,),
        in_specs=[
            one_head,
            one_head,
            pl.BlockSpec((all_keys, HD), lambda p: (0, p // HALF * 2)),
            pl.BlockSpec((all_keys, HD), lambda p: (0, p // HALF * 2 + 1)),
        ],
        out_specs=[pl.BlockSpec((all_keys, 2 * HD), lambda p: (0, p // HALF)), one_head],
        scratch_shapes=[
            pltpu.VMEM((all_keys, slots), F32),
            pltpu.VMEM((all_keys, slots), F32),
            pltpu.VMEM((all_keys, HD), F32),
            pltpu.VMEM((all_keys, HD), F32),
            pltpu.VMEM((all_keys, HD), F32),
            pltpu.VMEM((HD, all_keys), BF),
        ],
        compiler_params=params(),
        cost_estimate=pl.CostEstimate(
            flops=10 * HD * pairs,
            bytes_accessed=2 * (3 * slots * width_q + 2 * all_keys * width_kv),
            transcendentals=pairs,
        ),
        name="attend",
    )(home_q, home_g, all_kv, all_kv)

    kv_total = lax.psum_scatter(grad_kv, COLUMN, scatter_dimension=0, tiled=True)
    back_q = over_plane(grad_q)
    back_kv = over_plane(kv_total)

    out_q = pl.pallas_call(
        unpack_q_kernel,
        out_shape=struct(rows, width_q),
        grid_spec=pltpu.PrefetchScalarGridSpec(
            num_scalar_prefetch=1,
            grid=(QH,),
            in_specs=[whole, to_sorted],
            out_specs=from_slot,
            scratch_shapes=[pltpu.VMEM((rows, slots), BF)],
        ),
        compiler_params=params(),
        name="unpack_q",
    )(order, group_of_row, back_q)
    out_k, out_v = pl.pallas_call(
        unpack_kv_kernel,
        out_shape=(struct(rows, KVH * HD), struct(rows, KVH * HD)),
        compiler_params=params(),
        name="unpack_kv",
    )(group_of_row, back_kv)
    return out_q, out_k, out_v


def solution(mesh):
    fine = Mesh(mesh.devices.reshape(4, 4, 2, 2, 4), AXES)
    split = P(AXES, None)
    return jax.shard_map(
        per_device,
        mesh=fine,
        in_specs=(split, split, split, split, split, P()),
        out_specs=(split, split, split),
        check_vma=False,
    )
```

```python
import math

import jax
import jax.numpy as jnp
from jax import lax
from jax.experimental import pallas as pl
from jax.experimental.pallas import tpu as pltpu
from jax.sharding import Mesh
from jax.sharding import PartitionSpec as P

HD = 128
QH = 16
KVH = 2
GROUP_HEADS = 7
CAP = 8
HALF = QH // KVH
EMPTY = 64.0
NEG = -1e30
AXES = ("zh", "y", "c", "zl", "x")
PLANE = ("y", "c", "x")
COLUMN = ("zh", "zl")
BF = jnp.bfloat16
F32 = jnp.float32
KEY_TILE = 512
VMEM = 60 * 1024 * 1024


def contract_last(left, right):
    return lax.dot_general(left, right, (((1,), (1,)), ((), ())), preferred_element_type=F32)


def dot(left, right):
    return jnp.dot(left, right, preferred_element_type=F32)


def columns(at, width=HD):
    return pl.ds(pl.multiple_of(at * width, width), width)


def place_of(head):
    real = head < KVH * GROUP_HEADS
    return jnp.where(
        real,
        head + (head >= GROUP_HEADS).astype(jnp.int32),
        (head - KVH * GROUP_HEADS) * HALF + GROUP_HEADS,
    )


def row_groups(group_ref):
    rows = group_ref.shape[1]
    along = jnp.broadcast_to(group_ref[...].astype(F32), (rows, rows))
    across = along.T
    first = lax.broadcasted_iota(jnp.int32, (rows, rows), 0)
    second = lax.broadcasted_iota(jnp.int32, (rows, rows), 1)
    return along, across, along == across, first < second


def placer_of(group_ref, slots):
    rows = group_ref.shape[1]
    along, across, same, earlier = row_groups(group_ref)
    before = jnp.sum(jnp.where(same & earlier, 1.0, 0.0), axis=0, keepdims=True)
    target = (along[:1] * CAP + before).astype(jnp.int32)
    return jnp.where(lax.broadcasted_iota(jnp.int32, (slots, rows), 0) == target, 1.0, 0.0).astype(BF)


def taker_of(group_ref, slots):
    rows = group_ref.shape[1]
    along, across, same, earlier = row_groups(group_ref)
    later = lax.broadcasted_iota(jnp.int32, (rows, rows), 0) > lax.broadcasted_iota(
        jnp.int32, (rows, rows), 1
    )
    before = jnp.sum(jnp.where(same & later, 1.0, 0.0), axis=1, keepdims=True)
    target = (across[:, :1] * CAP + before).astype(jnp.int32)
    return jnp.where(lax.broadcasted_iota(jnp.int32, (rows, slots), 1) == target, 1.0, 0.0).astype(BF)


def pack_kv_kernel(group_ref, key_ref, value_ref, out_ref):
    slots = out_ref.shape[0]
    placer = placer_of(group_ref, slots)
    filled = jnp.sum(placer.astype(F32), axis=1, keepdims=True)
    lane = lax.broadcasted_iota(jnp.int32, (slots, HD), 1)
    mark = jnp.where((lane == 0) & (filled < 0.5), EMPTY, 0.0)
    for c in range(KVH):
        cols = slice(c * HD, (c + 1) * HD)
        out_ref[:, 2 * c * HD : (2 * c + 1) * HD] = dot(placer, key_ref[:, cols]).astype(BF)
        out_ref[:, (2 * c + 1) * HD : (2 * c + 2) * HD] = (dot(placer, value_ref[:, cols]) + mark).astype(BF)


def pack_qg_kernel(head_ref, group_ref, query_ref, grad_ref, out_ref):
    placer = placer_of(group_ref, out_ref.shape[0])
    for slot in range(QH):
        cols = slice(slot * HD, (slot + 1) * HD)
        head = head_ref[slot]
        place = place_of(head)
        real = (head < KVH * GROUP_HEADS).astype(F32)
        out_ref[:, columns(place)] = dot(placer, query_ref[:, cols]).astype(BF)
        out_ref[:, columns(QH + place)] = (dot(placer, grad_ref[:, cols]) * real).astype(BF)


def attend_kernel(qg_ref, kv_ref, dkv_ref, dq_ref, s_ref, p_ref, dk_ref, dv_ref, bias_ref, kt_ref):
    keys = kv_ref.shape[0]
    rows = qg_ref.shape[0]
    scale = HD ** (-0.5)
    unit = scale * math.log2(math.e)
    parts = [slice(t, t + KEY_TILE) for t in range(0, keys, KEY_TILE)]
    low = jnp.full((8, rows), -3e38, F32)

    def fold(tile):
        return tile.reshape(tile.shape[0] // 8, 8, rows)

    def one_key_head(c, _):
        k_cols, v_cols = columns(2 * c), columns(2 * c + 1)
        dk_ref[...] = jnp.zeros_like(dk_ref)
        dv_ref[...] = jnp.zeros_like(dv_ref)
        empty = kv_ref[:, v_cols][:, :1].astype(F32) > 0.5 * EMPTY
        bias_ref[...] = jnp.broadcast_to(jnp.where(empty, NEG, 0.0), bias_ref.shape)
        kt_ref[...] = kv_ref[:, k_cols].T

        def scores(buffer, q, part, top):
            bias = jnp.concatenate([bias_ref[part, :]] * (rows // HD), axis=1)
            s = contract_last(kv_ref[part, k_cols], q) + bias
            s_ref[buffer, part, :] = s
            return jnp.maximum(top, jnp.max(fold(s), axis=0))

        def one_head(h, top, here, there, last=False):
            at = c * HALF + h
            q = qg_ref[:, columns(at)]
            g = qg_ref[:, columns(QH + at)]
            top = jnp.max(top, axis=0, keepdims=True)
            total = jnp.zeros((8, rows), F32)
            cross = jnp.zeros((8, rows), F32)
            for part in parts:
                dp = contract_last(kv_ref[part, v_cols], g)
                e = jnp.exp2((s_ref[here, part, :] - top) * unit)
                s_ref[here, part, :] = e
                p_ref[part, :] = dp
                total = total + jnp.sum(fold(e), axis=0)
                cross = cross + jnp.sum(fold(e * dp), axis=0)
            share = 1.0 / jnp.sum(total, axis=0, keepdims=True)
            row_dot = jnp.sum(cross, axis=0, keepdims=True) * share
            dqt = jnp.zeros((HD, rows), F32)
            next_top = low
            if not last:
                next_q = qg_ref[:, columns(at + 1)]
            for part in parts:
                if not last:
                    next_top = scores(there, next_q, part, next_top)
                p = s_ref[here, part, :] * share
                ds = (p * (p_ref[part, :] - row_dot)).astype(BF)
                dv_ref[part, :] += dot(p.astype(BF), g)
                dk_ref[part, :] += dot(ds, q)
                dqt += dot(kt_ref[:, part], ds)
            dq_ref[:, columns(at)] = (dqt * scale).T.astype(BF)
            return next_top

        def two_heads(i, top):
            top = one_head(2 * i, top, 0, 1)
            return one_head(2 * i + 1, top, 1, 0)

        first_q = qg_ref[:, columns(c * HALF)]
        top = low
        for part in parts:
            top = scores(0, first_q, part, top)
        top = lax.fori_loop(0, HALF // 2 - 1, two_heads, top)
        top = one_head(HALF - 2, top, 0, 1)
        one_head(HALF - 1, top, 1, 0, last=True)
        dkv_ref[:, k_cols] = (dk_ref[...] * scale).astype(BF)
        dkv_ref[:, v_cols] = dv_ref[...].astype(BF)
        return 0

    lax.fori_loop(0, KVH, one_key_head, 0)


def unpack_q_kernel(head_ref, group_ref, dq_ref, out_ref):
    taker = taker_of(group_ref, dq_ref.shape[0])
    for slot in range(QH):
        place = place_of(head_ref[slot])
        out_ref[:, slot * HD : (slot + 1) * HD] = dot(taker, dq_ref[:, columns(place)]).astype(BF)


def unpack_kv_kernel(group_ref, dkv_ref, dk_ref, dv_ref):
    taker = taker_of(group_ref, dkv_ref.shape[0])
    for c in range(KVH):
        cols = slice(c * HD, (c + 1) * HD)
        dk_ref[:, cols] = dot(taker, dkv_ref[:, 2 * c * HD : (2 * c + 1) * HD]).astype(BF)
        dv_ref[:, cols] = dot(taker, dkv_ref[:, (2 * c + 1) * HD : (2 * c + 2) * HD]).astype(BF)


def struct(*shape):
    return jax.ShapeDtypeStruct(shape, BF)


def call(kernel, name, out_shape, scalars=0, inputs=1, scratch=(), cost=None):
    whole = pl.BlockSpec(memory_space=pltpu.VMEM)
    many = isinstance(out_shape, tuple)
    return pl.pallas_call(
        kernel,
        out_shape=out_shape,
        in_specs=[pl.BlockSpec(memory_space=pltpu.SMEM)] * scalars + [whole] * inputs,
        out_specs=(whole,) * len(out_shape) if many else whole,
        scratch_shapes=scratch,
        compiler_params=pltpu.CompilerParams(vmem_limit_bytes=VMEM),
        cost_estimate=cost,
        name=name,
    )


def per_device(queries, keys, values, grad_out, group_of_row, head_slot):
    rows = queries.shape[0]
    groups = lax.axis_size(PLANE)
    column = lax.axis_size(COLUMN)
    slots = groups * CAP
    width_q = QH * HD
    width_kv = 2 * KVH * HD
    all_keys = column * slots
    row_group = group_of_row.reshape(1, rows)

    def over_plane(array):
        return lax.all_to_all(array, PLANE, split_axis=0, concat_axis=0, tiled=True)

    sent_kv = call(pack_kv_kernel, "pack_kv", struct(slots, width_kv), inputs=3)(row_group, keys, values)
    home_kv = over_plane(sent_kv)
    all_kv = lax.all_gather(home_kv, COLUMN, axis=0, tiled=True)
    sent_qg = call(pack_qg_kernel, "pack_qg", struct(slots, 2 * width_q), scalars=1, inputs=3)(
        head_slot, row_group, queries, grad_out
    )
    home_qg = over_plane(sent_qg)

    pairs = QH * slots * all_keys
    grad_kv, grad_q = call(
        attend_kernel,
        "attend",
        (struct(all_keys, width_kv), struct(slots, width_q)),
        inputs=2,
        scratch=[
            pltpu.VMEM((2, all_keys, slots), F32),
            pltpu.VMEM((all_keys, slots), F32),
            pltpu.VMEM((all_keys, HD), F32),
            pltpu.VMEM((all_keys, HD), F32),
            pltpu.VMEM((all_keys, HD), F32),
            pltpu.VMEM((HD, all_keys), BF),
        ],
        cost=pl.CostEstimate(
            flops=10 * HD * pairs,
            bytes_accessed=2 * (3 * slots * width_q + 2 * all_keys * width_kv),
            transcendentals=pairs,
        ),
    )(home_qg, all_kv)

    kv_total = lax.psum_scatter(grad_kv, COLUMN, scatter_dimension=0, tiled=True)
    back_q = over_plane(grad_q)
    back_kv = over_plane(kv_total)
    out_q = call(unpack_q_kernel, "unpack_q", struct(rows, width_q), scalars=1, inputs=2)(
        head_slot, row_group, back_q
    )
    out_k, out_v = call(
        unpack_kv_kernel, "unpack_kv", (struct(rows, KVH * HD), struct(rows, KVH * HD)), inputs=2
    )(row_group, back_kv)
    return out_q, out_k, out_v


def solution(mesh):
    fine = Mesh(mesh.devices.reshape(4, 4, 2, 2, 4), AXES)
    split = P(AXES, None)
    return jax.shard_map(
        per_device,
        mesh=fine,
        in_specs=(split, split, split, split, split, P()),
        out_specs=(split, split, split),
        check_vma=False,
    )
```

```python
import math

import jax
import jax.numpy as jnp
from jax import lax
from jax.experimental import pallas as pl
from jax.experimental.pallas import tpu as pltpu
from jax.sharding import Mesh
from jax.sharding import PartitionSpec as P

HD = 128
QH = 16
KVH = 2
GROUP_HEADS = 7
CAP = 8
HALF = QH // KVH
EMPTY = 64.0
NEG = -1e30
AXES = ("zh", "y", "c", "zl", "x")
PLANE = ("y", "c", "x")
COLUMN = ("zh", "zl")
BF = jnp.bfloat16
F32 = jnp.float32
KEY_TILE = 512
VMEM = 60 * 1024 * 1024


def contract_last(left, right):
    return lax.dot_general(left, right, (((1,), (1,)), ((), ())), preferred_element_type=F32)


def dot(left, right):
    return jnp.dot(left, right, preferred_element_type=F32)


def columns(at, width=HD):
    return pl.ds(pl.multiple_of(at * width, width), width)


def place_of(head):
    real = head < KVH * GROUP_HEADS
    return jnp.where(
        real,
        head + (head >= GROUP_HEADS).astype(jnp.int32),
        (head - KVH * GROUP_HEADS) * HALF + GROUP_HEADS,
    )


def row_groups(group_ref):
    rows = group_ref.shape[1]
    along = jnp.broadcast_to(group_ref[...].astype(F32), (rows, rows))
    across = along.T
    first = lax.broadcasted_iota(jnp.int32, (rows, rows), 0)
    second = lax.broadcasted_iota(jnp.int32, (rows, rows), 1)
    return along, across, along == across, first < second


def placer_of(group_ref, slots):
    rows = group_ref.shape[1]
    along, across, same, earlier = row_groups(group_ref)
    before = jnp.sum(jnp.where(same & earlier, 1.0, 0.0), axis=0, keepdims=True)
    target = (along[:1] * CAP + before).astype(jnp.int32)
    return jnp.where(lax.broadcasted_iota(jnp.int32, (slots, rows), 0) == target, 1.0, 0.0).astype(BF)


def taker_of(group_ref, slots):
    rows = group_ref.shape[1]
    along, across, same, earlier = row_groups(group_ref)
    later = lax.broadcasted_iota(jnp.int32, (rows, rows), 0) > lax.broadcasted_iota(
        jnp.int32, (rows, rows), 1
    )
    before = jnp.sum(jnp.where(same & later, 1.0, 0.0), axis=1, keepdims=True)
    target = (across[:, :1] * CAP + before).astype(jnp.int32)
    return jnp.where(lax.broadcasted_iota(jnp.int32, (rows, slots), 1) == target, 1.0, 0.0).astype(BF)


def pack_kv_kernel(group_ref, key_ref, value_ref, out_ref):
    slots = out_ref.shape[0]
    placer = placer_of(group_ref, slots)
    filled = jnp.sum(placer.astype(F32), axis=1, keepdims=True)
    lane = lax.broadcasted_iota(jnp.int32, (slots, HD), 1)
    mark = jnp.where((lane == 0) & (filled < 0.5), EMPTY, 0.0)
    for c in range(KVH):
        cols = slice(c * HD, (c + 1) * HD)
        out_ref[:, 2 * c * HD : (2 * c + 1) * HD] = dot(placer, key_ref[:, cols]).astype(BF)
        out_ref[:, (2 * c + 1) * HD : (2 * c + 2) * HD] = (dot(placer, value_ref[:, cols]) + mark).astype(BF)


def pack_qg_kernel(head_ref, group_ref, query_ref, grad_ref, out_ref):
    placer = placer_of(group_ref, out_ref.shape[0])
    for slot in range(QH):
        cols = slice(slot * HD, (slot + 1) * HD)
        head = head_ref[slot]
        place = place_of(head)
        real = (head < KVH * GROUP_HEADS).astype(F32)
        out_ref[:, columns(place)] = dot(placer, query_ref[:, cols]).astype(BF)
        out_ref[:, columns(QH + place)] = (dot(placer, grad_ref[:, cols]) * real).astype(BF)


def attend_kernel(*refs):
    qg_ref, kv_refs, dkv_refs, dq_ref = refs[0], refs[1:10], refs[10:19], refs[19]
    k_ref, v_ref, s_ref, p_ref, dk_ref, dv_ref, bias_ref, kt_ref = refs[20:]
    keys = k_ref.shape[0]
    rows = qg_ref.shape[0]
    block = keys // 8
    scale = HD ** (-0.5)
    unit = scale * math.log2(math.e)
    parts = [slice(t, t + KEY_TILE) for t in range(0, keys, KEY_TILE)]
    low = jnp.full((8, rows), -3e38, F32)

    def fold(tile):
        return tile.reshape(tile.shape[0] // 8, 8, rows)

    def one_key_head(c):
        for i in range(8):
            here = slice(i * block, (i + 1) * block)
            ref, first = (kv_refs[i], 2 * c * HD) if i < 7 else (kv_refs[7 + c], 0)
            k_ref[here, :] = ref[:, first : first + HD]
            v_ref[here, :] = ref[:, first + HD : first + 2 * HD]
        dk_ref[...] = jnp.zeros_like(dk_ref)
        dv_ref[...] = jnp.zeros_like(dv_ref)
        empty = v_ref[:, :1].astype(F32) > 0.5 * EMPTY
        bias_ref[...] = jnp.broadcast_to(jnp.where(empty, NEG, 0.0), bias_ref.shape)
        kt_ref[...] = k_ref[...].T

        def scores(buffer, q, part, top):
            bias = jnp.concatenate([bias_ref[part, :]] * (rows // HD), axis=1)
            s = contract_last(k_ref[part, :], q) + bias
            s_ref[buffer, part, :] = s
            return jnp.maximum(top, jnp.max(fold(s), axis=0))

        def one_head(h, top, here, there, last=False):
            at = c * HALF + h
            q = qg_ref[:, columns(at)]
            g = qg_ref[:, columns(QH + at)]
            top = jnp.max(top, axis=0, keepdims=True)
            total = jnp.zeros((8, rows), F32)
            cross = jnp.zeros((8, rows), F32)
            for part in parts:
                dp = contract_last(v_ref[part, :], g)
                e = jnp.exp2((s_ref[here, part, :] - top) * unit)
                s_ref[here, part, :] = e
                p_ref[part, :] = dp
                total = total + jnp.sum(fold(e), axis=0)
                cross = cross + jnp.sum(fold(e * dp), axis=0)
            share = 1.0 / jnp.sum(total, axis=0, keepdims=True)
            row_dot = jnp.sum(cross, axis=0, keepdims=True) * share
            dqt = jnp.zeros((HD, rows), F32)
            next_top = low
            if not last:
                next_q = qg_ref[:, columns(at + 1)]
            for part in parts:
                if not last:
                    next_top = scores(there, next_q, part, next_top)
                p = s_ref[here, part, :] * share
                ds = (p * (p_ref[part, :] - row_dot)).astype(BF)
                dv_ref[part, :] += dot(p.astype(BF), g)
                dk_ref[part, :] += dot(ds, q)
                dqt += dot(kt_ref[:, part], ds)
            dq_ref[:, columns(at)] = (dqt * scale).T.astype(BF)
            return next_top

        def two_heads(i, top):
            top = one_head(2 * i, top, 0, 1)
            return one_head(2 * i + 1, top, 1, 0)

        first_q = qg_ref[:, columns(c * HALF)]
        top = low
        for part in parts:
            top = scores(0, first_q, part, top)
        top = lax.fori_loop(0, HALF // 2 - 1, two_heads, top)
        top = one_head(HALF - 2, top, 0, 1)
        one_head(HALF - 1, top, 1, 0, last=True)
        for i in range(8):
            here = slice(i * block, (i + 1) * block)
            ref, first = (dkv_refs[i], 2 * c * HD) if i < 7 else (dkv_refs[7 + c], 0)
            ref[:, first : first + HD] = (dk_ref[here, :] * scale).astype(BF)
            ref[:, first + HD : first + 2 * HD] = dv_ref[here, :].astype(BF)

    for c in range(KVH):
        one_key_head(c)


def unpack_q_kernel(head_ref, group_ref, dq_ref, out_ref):
    taker = taker_of(group_ref, dq_ref.shape[0])
    for slot in range(QH):
        place = place_of(head_ref[slot])
        out_ref[:, slot * HD : (slot + 1) * HD] = dot(taker, dq_ref[:, columns(place)]).astype(BF)


def unpack_kv_kernel(group_ref, dkv_ref, dk_ref, dv_ref):
    taker = taker_of(group_ref, dkv_ref.shape[0])
    for c in range(KVH):
        cols = slice(c * HD, (c + 1) * HD)
        dk_ref[:, cols] = dot(taker, dkv_ref[:, 2 * c * HD : (2 * c + 1) * HD]).astype(BF)
        dv_ref[:, cols] = dot(taker, dkv_ref[:, (2 * c + 1) * HD : (2 * c + 2) * HD]).astype(BF)


def ring_steps(axis):
    size = lax.axis_size(axis)
    up = [(i, (i + 1) % size) for i in range(size)]
    down = [(i, (i - 1) % size) for i in range(size)]
    return lambda x: lax.ppermute(x, axis, up), lambda x: lax.ppermute(x, axis, down)


def gather_column(block):
    up, down = ring_steps(COLUMN)
    half = block.shape[1] // 2
    below = above = block
    blocks = [block]
    for _ in range(3):
        below, above = up(below), down(above)
        blocks += [below, above]
    return blocks + [up(below[:, :half]), down(above[:, half:])]


def scatter_column(blocks):
    up, down = ring_steps(COLUMN)

    def plus(*terms):
        return sum(term.astype(F32) for term in terms).astype(BF)

    own, to_below, to_above = blocks[0], blocks[1:7:2], blocks[2:7:2]
    zeros = jnp.zeros_like(blocks[7])
    rising = plus(to_above[2], jnp.concatenate([up(blocks[7]), zeros], axis=1))
    falling = plus(to_below[2], jnp.concatenate([zeros, down(blocks[8])], axis=1))
    for i in (1, 0):
        rising, falling = plus(to_above[i], up(rising)), plus(to_below[i], down(falling))
    return plus(own, up(rising), down(falling))


def struct(*shape):
    return jax.ShapeDtypeStruct(shape, BF)


def call(kernel, name, out_shape, scalars=0, inputs=1, scratch=(), cost=None):
    whole = pl.BlockSpec(memory_space=pltpu.VMEM)
    many = isinstance(out_shape, tuple)
    return pl.pallas_call(
        kernel,
        out_shape=out_shape,
        in_specs=[pl.BlockSpec(memory_space=pltpu.SMEM)] * scalars + [whole] * inputs,
        out_specs=(whole,) * len(out_shape) if many else whole,
        scratch_shapes=scratch,
        compiler_params=pltpu.CompilerParams(vmem_limit_bytes=VMEM),
        cost_estimate=cost,
        name=name,
    )


def per_device(queries, keys, values, grad_out, group_of_row, head_slot):
    rows = queries.shape[0]
    groups = lax.axis_size(PLANE)
    column = lax.axis_size(COLUMN)
    slots = groups * CAP
    width_q = QH * HD
    width_kv = 2 * KVH * HD
    all_keys = column * slots
    row_group = group_of_row.reshape(1, rows)

    def over_plane(array):
        return lax.all_to_all(array, PLANE, split_axis=0, concat_axis=0, tiled=True)

    sent_kv = call(pack_kv_kernel, "pack_kv", struct(slots, width_kv), inputs=3)(row_group, keys, values)
    home_kv = over_plane(sent_kv)
    all_kv = gather_column(home_kv)
    sent_qg = call(pack_qg_kernel, "pack_qg", struct(slots, 2 * width_q), scalars=1, inputs=3)(
        head_slot, row_group, queries, grad_out
    )
    home_qg = over_plane(sent_qg)

    pairs = QH * slots * all_keys
    blocks = [struct(*block.shape) for block in all_kv]
    *grad_kv, grad_q = call(
        attend_kernel,
        "attend",
        (*blocks, struct(slots, width_q)),
        inputs=1 + len(all_kv),
        scratch=[
            pltpu.VMEM((all_keys, HD), BF),
            pltpu.VMEM((all_keys, HD), BF),
            pltpu.VMEM((2, all_keys, slots), F32),
            pltpu.VMEM((all_keys, slots), F32),
            pltpu.VMEM((all_keys, HD), F32),
            pltpu.VMEM((all_keys, HD), F32),
            pltpu.VMEM((all_keys, HD), F32),
            pltpu.VMEM((HD, all_keys), BF),
        ],
        cost=pl.CostEstimate(
            flops=10 * HD * pairs,
            bytes_accessed=2 * (3 * slots * width_q + 2 * all_keys * width_kv),
            transcendentals=pairs,
        ),
    )(home_qg, *all_kv)

    kv_total = scatter_column(grad_kv)
    back_q = over_plane(grad_q)
    back_kv = over_plane(kv_total)
    out_q = call(unpack_q_kernel, "unpack_q", struct(rows, width_q), scalars=1, inputs=2)(
        head_slot, row_group, back_q
    )
    out_k, out_v = call(
        unpack_kv_kernel, "unpack_kv", (struct(rows, KVH * HD), struct(rows, KVH * HD)), inputs=2
    )(row_group, back_kv)
    return out_q, out_k, out_v


def solution(mesh):
    fine = Mesh(mesh.devices.reshape(4, 4, 2, 2, 4), AXES)
    split = P(AXES, None)
    return jax.shard_map(
        per_device,
        mesh=fine,
        in_specs=(split, split, split, split, split, P()),
        out_specs=(split, split, split),
        check_vma=False,
    )
```

```python
import math

import jax
import jax.numpy as jnp
from jax import lax
from jax.experimental import pallas as pl
from jax.experimental.pallas import tpu as pltpu
from jax.sharding import Mesh
from jax.sharding import PartitionSpec as P

HD = 128
QH = 16
KVH = 2
GROUP_HEADS = 7
CAP = 8
HALF = QH // KVH
EMPTY = 64.0
NEG = -1e30
AXES = ("zh", "y", "c", "zl", "x")
PLANE = ("y", "c", "x")
COLUMN = ("zh", "zl")
BF = jnp.bfloat16
F32 = jnp.float32
KEY_TILE = 512
VMEM = 60 * 1024 * 1024


def contract_last(left, right):
    return lax.dot_general(left, right, (((1,), (1,)), ((), ())), preferred_element_type=F32)


def dot(left, right):
    return jnp.dot(left, right, preferred_element_type=F32)


def columns(at, width=HD):
    return pl.ds(pl.multiple_of(at * width, width), width)


def place_of(head):
    real = head < KVH * GROUP_HEADS
    return jnp.where(
        real,
        head + (head >= GROUP_HEADS).astype(jnp.int32),
        (head - KVH * GROUP_HEADS) * HALF + GROUP_HEADS,
    )


def row_groups(group_ref):
    rows = group_ref.shape[1]
    along = jnp.broadcast_to(group_ref[...].astype(F32), (rows, rows))
    across = along.T
    first = lax.broadcasted_iota(jnp.int32, (rows, rows), 0)
    second = lax.broadcasted_iota(jnp.int32, (rows, rows), 1)
    return along, across, along == across, first < second


def placer_of(group_ref, slots):
    rows = group_ref.shape[1]
    along, across, same, earlier = row_groups(group_ref)
    before = jnp.sum(jnp.where(same & earlier, 1.0, 0.0), axis=0, keepdims=True)
    target = (along[:1] * CAP + before).astype(jnp.int32)
    return jnp.where(lax.broadcasted_iota(jnp.int32, (slots, rows), 0) == target, 1.0, 0.0).astype(BF)


def taker_of(group_ref, slots):
    rows = group_ref.shape[1]
    along, across, same, earlier = row_groups(group_ref)
    later = lax.broadcasted_iota(jnp.int32, (rows, rows), 0) > lax.broadcasted_iota(
        jnp.int32, (rows, rows), 1
    )
    before = jnp.sum(jnp.where(same & later, 1.0, 0.0), axis=1, keepdims=True)
    target = (across[:, :1] * CAP + before).astype(jnp.int32)
    return jnp.where(lax.broadcasted_iota(jnp.int32, (rows, slots), 1) == target, 1.0, 0.0).astype(BF)


def pack_kv_kernel(group_ref, key_ref, value_ref, out_ref):
    slots = out_ref.shape[0]
    placer = placer_of(group_ref, slots)
    filled = jnp.sum(placer.astype(F32), axis=1, keepdims=True)
    lane = lax.broadcasted_iota(jnp.int32, (slots, HD), 1)
    mark = jnp.where((lane == 0) & (filled < 0.5), EMPTY, 0.0)
    for c in range(KVH):
        cols = slice(c * HD, (c + 1) * HD)
        out_ref[:, 2 * c * HD : (2 * c + 1) * HD] = dot(placer, key_ref[:, cols]).astype(BF)
        out_ref[:, (2 * c + 1) * HD : (2 * c + 2) * HD] = (dot(placer, value_ref[:, cols]) + mark).astype(BF)


def pack_qg_kernel(head_ref, group_ref, query_ref, grad_ref, out_ref):
    placer = placer_of(group_ref, out_ref.shape[0])
    for slot in range(QH):
        cols = slice(slot * HD, (slot + 1) * HD)
        head = head_ref[slot]
        place = place_of(head)
        real = (head < KVH * GROUP_HEADS).astype(F32)
        out_ref[:, columns(place)] = dot(placer, query_ref[:, cols]).astype(BF)
        out_ref[:, columns(QH + place)] = (dot(placer, grad_ref[:, cols]) * real).astype(BF)


def attend_kernel(*refs):
    qg_ref, kv_refs, dkv_refs, dq_ref = refs[0], refs[1:10], refs[10:19], refs[19]
    kv_ref, x_ref, y_ref, p_ref, dk_ref, dv_ref, bias_ref, kt_ref = refs[20:]
    keys = kv_ref.shape[0]
    rows = qg_ref.shape[0]
    block = keys // 8
    scale = HD ** (-0.5)
    unit = scale * math.log2(math.e)
    parts = [slice(t, t + KEY_TILE) for t in range(0, keys, KEY_TILE)]
    low = jnp.full((8, rows), -3e38, F32)
    zero = jnp.zeros((8, rows), F32)

    def fold(tile):
        return tile.reshape(tile.shape[0] // 8, 8, rows)

    for i in range(8):
        here = slice(i * block, (i + 1) * block)
        for c in range(KVH):
            cols = slice(2 * c * HD, 2 * (c + 1) * HD)
            kv_ref[here, cols] = kv_refs[i][:, cols] if i < 7 else kv_refs[7 + c][...]
    dk_ref[...] = jnp.zeros_like(dk_ref)
    dv_ref[...] = jnp.zeros_like(dv_ref)
    for c in range(KVH):
        empty = kv_ref[:, (2 * c + 1) * HD : (2 * c + 1) * HD + 1].astype(F32) > 0.5 * EMPTY
        bias_ref[c] = jnp.broadcast_to(jnp.where(empty, NEG, 0.0), (keys, HD))
        kt_ref[c] = kv_ref[:, 2 * c * HD : (2 * c + 1) * HD].T

    def key_head(h):
        return int(h >= HALF) if isinstance(h, int) else (h >= HALF).astype(jnp.int32)

    def scores(h, part, top):
        c = key_head(h)
        bias = jnp.concatenate([bias_ref[c, part, :]] * (rows // HD), axis=1)
        x = contract_last(kv_ref[part, columns(2 * c)], qg_ref[:, columns(h)]) + bias
        x_ref[part, :] = x
        return jnp.maximum(top, jnp.max(fold(x), axis=0))

    def weights(h, part, top, total, cross):
        dp = contract_last(kv_ref[part, columns(2 * key_head(h) + 1)], qg_ref[:, columns(QH + h)])
        e = jnp.exp2((x_ref[part, :] - top) * unit)
        y_ref[part, :] = e
        p_ref[part, :] = dp
        return total + jnp.sum(fold(e), axis=0), cross + jnp.sum(fold(e * dp), axis=0)

    def gradients(h, part, q, g, share, row_dot, dqt):
        c = key_head(h)
        p = y_ref[part, :] * share
        ds = (p * (p_ref[part, :] - row_dot)).astype(BF)
        dv_ref[c, part, :] += dot(p.astype(BF), g)
        dk_ref[c, part, :] += dot(ds, q)
        return dqt + dot(kt_ref[c, :, part], ds)

    def step(i, top, total, cross):
        known = not isinstance(i, int)
        has_gradients = known or i >= 0
        has_weights = known or 0 <= i + 1 < QH
        has_scores = known or i + 2 < QH
        top = jnp.max(top, axis=0, keepdims=True)
        if has_gradients:
            share = 1.0 / jnp.sum(total, axis=0, keepdims=True)
            row_dot = jnp.sum(cross, axis=0, keepdims=True) * share
            q, g = qg_ref[:, columns(i)], qg_ref[:, columns(QH + i)]
        dqt = jnp.zeros((HD, rows), F32)
        next_top, next_total, next_cross = low, zero, zero
        for part in parts:
            if has_gradients:
                dqt = gradients(i, part, q, g, share, row_dot, dqt)
            if has_weights:
                next_total, next_cross = weights(i + 1, part, top, next_total, next_cross)
            if has_scores:
                next_top = scores(i + 2, part, next_top)
        if has_gradients:
            dq_ref[:, columns(i)] = (dqt * scale).T.astype(BF)
        return next_top, next_total, next_cross

    state = step(-1, *step(-2, low, zero, zero))
    state = lax.fori_loop(0, QH - 2, lambda i, state: step(i, *state), state)
    step(QH - 1, *step(QH - 2, *state))

    for i in range(8):
        here = slice(i * block, (i + 1) * block)
        for c in range(KVH):
            ref, first = (dkv_refs[i], 2 * c * HD) if i < 7 else (dkv_refs[7 + c], 0)
            ref[:, first : first + HD] = (dk_ref[c, here, :] * scale).astype(BF)
            ref[:, first + HD : first + 2 * HD] = dv_ref[c, here, :].astype(BF)


def unpack_q_kernel(head_ref, group_ref, dq_ref, out_ref, taker_ref):
    taker = taker_of(group_ref, dq_ref.shape[0])
    taker_ref[...] = taker
    for slot in range(QH):
        place = place_of(head_ref[slot])
        out_ref[:, slot * HD : (slot + 1) * HD] = dot(taker, dq_ref[:, columns(place)]).astype(BF)


def unpack_kv_kernel(taker_ref, dkv_ref, dk_ref, dv_ref):
    rows = dot(taker_ref[...], dkv_ref[...]).astype(BF)
    for c in range(KVH):
        cols = slice(c * HD, (c + 1) * HD)
        dk_ref[:, cols] = rows[:, 2 * c * HD : (2 * c + 1) * HD]
        dv_ref[:, cols] = rows[:, (2 * c + 1) * HD : (2 * c + 2) * HD]


def step_by(axis, distance):
    size = lax.axis_size(axis)
    pairs = [(i, (i + distance) % size) for i in range(size)]
    return lambda x: lax.ppermute(x, axis, pairs)


def gather_column(block):
    up, down = step_by(COLUMN, 1), step_by(COLUMN, -1)
    half = block.shape[1] // 2
    below = above = block
    blocks = [block]
    for i in range(3):
        if i == 2:
            far = [
                step_by(COLUMN, 2)(below[:, :half]),
                step_by(COLUMN, -2)(above[:, half:]),
            ]
        below, above = up(below), down(above)
        blocks += [below, above]
    return blocks + far


def scatter_column(blocks):
    up, down = step_by(COLUMN, 1), step_by(COLUMN, -1)

    def plus(*terms):
        return sum(term.astype(F32) for term in terms).astype(BF)

    own, to_below, to_above = blocks[0], blocks[1:7:2], blocks[2:7:2]
    zeros = jnp.zeros_like(blocks[7])
    far_up = jnp.concatenate([step_by(COLUMN, 2)(blocks[7]), zeros], axis=1)
    far_down = jnp.concatenate([zeros, step_by(COLUMN, -2)(blocks[8])], axis=1)
    rising = plus(to_above[1], up(to_above[2]), far_up)
    falling = plus(to_below[1], down(to_below[2]), far_down)
    rising, falling = plus(to_above[0], up(rising)), plus(to_below[0], down(falling))
    return plus(own, up(rising), down(falling))


def struct(*shape):
    return jax.ShapeDtypeStruct(shape, BF)


def call(kernel, name, out_shape, scalars=0, inputs=1, scratch=(), cost=None):
    whole = pl.BlockSpec(memory_space=pltpu.VMEM)
    many = isinstance(out_shape, tuple)
    return pl.pallas_call(
        kernel,
        out_shape=out_shape,
        in_specs=[pl.BlockSpec(memory_space=pltpu.SMEM)] * scalars + [whole] * inputs,
        out_specs=(whole,) * len(out_shape) if many else whole,
        scratch_shapes=scratch,
        compiler_params=pltpu.CompilerParams(vmem_limit_bytes=VMEM),
        cost_estimate=cost,
        name=name,
    )


def per_device(queries, keys, values, grad_out, group_of_row, head_slot):
    rows = queries.shape[0]
    groups = lax.axis_size(PLANE)
    column = lax.axis_size(COLUMN)
    slots = groups * CAP
    width_q = QH * HD
    width_kv = 2 * KVH * HD
    all_keys = column * slots
    row_group = group_of_row.reshape(1, rows)

    def over_plane(array):
        return lax.all_to_all(array, PLANE, split_axis=0, concat_axis=0, tiled=True)

    sent_kv = call(pack_kv_kernel, "pack_kv", struct(slots, width_kv), inputs=3)(row_group, keys, values)
    home_kv = over_plane(sent_kv)
    all_kv = gather_column(home_kv)
    sent_qg = call(pack_qg_kernel, "pack_qg", struct(slots, 2 * width_q), scalars=1, inputs=3)(
        head_slot, row_group, queries, grad_out
    )
    home_qg = over_plane(sent_qg)

    pairs = QH * slots * all_keys
    blocks = [struct(*block.shape) for block in all_kv]
    *grad_kv, grad_q = call(
        attend_kernel,
        "attend",
        (*blocks, struct(slots, width_q)),
        inputs=1 + len(all_kv),
        scratch=[
            pltpu.VMEM((all_keys, width_kv), BF),
            pltpu.VMEM((all_keys, slots), F32),
            pltpu.VMEM((all_keys, slots), F32),
            pltpu.VMEM((all_keys, slots), F32),
            pltpu.VMEM((KVH, all_keys, HD), F32),
            pltpu.VMEM((KVH, all_keys, HD), F32),
            pltpu.VMEM((KVH, all_keys, HD), F32),
            pltpu.VMEM((KVH, HD, all_keys), BF),
        ],
        cost=pl.CostEstimate(
            flops=10 * HD * pairs,
            bytes_accessed=2 * (3 * slots * width_q + 2 * all_keys * width_kv),
            transcendentals=pairs,
        ),
    )(home_qg, *all_kv)

    kv_total = scatter_column(grad_kv)
    back_q = over_plane(grad_q)
    back_kv = over_plane(kv_total)
    out_q, taker = call(
        unpack_q_kernel, "unpack_q", (struct(rows, width_q), struct(rows, slots)), scalars=1, inputs=2
    )(head_slot, row_group, back_q)
    out_k, out_v = call(
        unpack_kv_kernel, "unpack_kv", (struct(rows, KVH * HD), struct(rows, KVH * HD)), inputs=2
    )(taker, back_kv)
    return out_q, out_k, out_v


def solution(mesh):
    fine = Mesh(mesh.devices.reshape(4, 4, 2, 2, 4), AXES)
    split = P(AXES, None)
    return jax.shard_map(
        per_device,
        mesh=fine,
        in_specs=(split, split, split, split, split, P()),
        out_specs=(split, split, split),
        check_vma=False,
    )
```

```python
import math

import jax
import jax.numpy as jnp
from jax import lax
from jax.experimental import pallas as pl
from jax.experimental.pallas import tpu as pltpu
from jax.sharding import Mesh
from jax.sharding import PartitionSpec as P

HD = 128
QH = 16
KVH = 2
GROUP_HEADS = 7
CAP = 8
HALF = QH // KVH
EMPTY = 64.0
NEG = -1e30
AXES = ("zh", "y", "c", "zl", "x")
PLANE = ("y", "c", "x")
COLUMN = ("zh", "zl")
BF = jnp.bfloat16
F32 = jnp.float32
KEY_TILE = 2048
CHUNK = 64
MIB = 1024 * 1024


def contract_last(left, right):
    return lax.dot_general(left, right, (((1,), (1,)), ((), ())), preferred_element_type=F32)


def dot(left, right):
    return jnp.dot(left, right, preferred_element_type=F32)


def columns(at, width=HD):
    return pl.ds(pl.multiple_of(at * width, width), width)


def place_of(head):
    real = head < KVH * GROUP_HEADS
    return jnp.where(
        real,
        head + (head >= GROUP_HEADS).astype(jnp.int32),
        (head - KVH * GROUP_HEADS) * HALF + GROUP_HEADS,
    )


def row_groups(group_ref):
    rows = group_ref.shape[1]
    along = jnp.broadcast_to(group_ref[...].astype(F32), (rows, rows))
    across = along.T
    first = lax.broadcasted_iota(jnp.int32, (rows, rows), 0)
    second = lax.broadcasted_iota(jnp.int32, (rows, rows), 1)
    return along, across, along == across, first < second


def placer_of(group_ref, slots):
    rows = group_ref.shape[1]
    along, across, same, earlier = row_groups(group_ref)
    before = jnp.sum(jnp.where(same & earlier, 1.0, 0.0), axis=0, keepdims=True)
    target = (along[:1] * CAP + before).astype(jnp.int32)
    return jnp.where(lax.broadcasted_iota(jnp.int32, (slots, rows), 0) == target, 1.0, 0.0).astype(BF)


def taker_of(group_ref, slots):
    rows = group_ref.shape[1]
    along, across, same, earlier = row_groups(group_ref)
    later = lax.broadcasted_iota(jnp.int32, (rows, rows), 0) > lax.broadcasted_iota(
        jnp.int32, (rows, rows), 1
    )
    before = jnp.sum(jnp.where(same & later, 1.0, 0.0), axis=1, keepdims=True)
    target = (across[:, :1] * CAP + before).astype(jnp.int32)
    return jnp.where(lax.broadcasted_iota(jnp.int32, (rows, slots), 1) == target, 1.0, 0.0).astype(BF)


def pack_kv_kernel(group_ref, key_ref, value_ref, out_ref):
    slots = out_ref.shape[0]
    placer = placer_of(group_ref, slots)
    filled = jnp.sum(placer.astype(F32), axis=1, keepdims=True)
    lane = lax.broadcasted_iota(jnp.int32, (slots, HD), 1)
    mark = jnp.where((lane == 0) & (filled < 0.5), EMPTY, 0.0)
    for c in range(KVH):
        cols = slice(c * HD, (c + 1) * HD)
        out_ref[:, 2 * c * HD : (2 * c + 1) * HD] = dot(placer, key_ref[:, cols]).astype(BF)
        out_ref[:, (2 * c + 1) * HD : (2 * c + 2) * HD] = (dot(placer, value_ref[:, cols]) + mark).astype(BF)


def pack_qg_kernel(head_ref, group_ref, query_ref, grad_ref, out_ref):
    placer = placer_of(group_ref, out_ref.shape[0])
    for slot in range(QH):
        cols = slice(slot * HD, (slot + 1) * HD)
        head = head_ref[slot]
        place = place_of(head)
        real = (head < KVH * GROUP_HEADS).astype(F32)
        out_ref[:, columns(place)] = dot(placer, query_ref[:, cols]).astype(BF)
        out_ref[:, columns(QH + place)] = (dot(placer, grad_ref[:, cols]) * real).astype(BF)


def attend_kernel(*refs):
    source_refs, dkv_refs, dq_ref = refs[:10], refs[10:19], refs[19]
    qg_ref, kv_ref, x_ref, y_ref, p_ref, dk_ref, dv_ref, bias_ref, kt_ref, sems = refs[20:]
    keys = kv_ref.shape[0]
    rows = qg_ref.shape[0]
    block = keys // 8
    scale = HD ** (-0.5)
    unit = scale * math.log2(math.e)
    parts = [slice(t, t + KEY_TILE) for t in range(0, keys, KEY_TILE)]
    chunks = range(0, KEY_TILE, CHUNK)
    low = jnp.full((8, rows), -3e38, F32)
    zero = jnp.zeros((8, rows), F32)

    def fold(tile):
        return tile.reshape(tile.shape[0] // 8, 8, rows)

    targets = [kv_ref.at[i * block : (i + 1) * block, :] for i in range(7)]
    targets += [kv_ref.at[7 * block :, : 2 * HD], kv_ref.at[7 * block :, 2 * HD :], qg_ref]
    fetches = [
        pltpu.make_async_copy(source, target, sems.at[i])
        for i, (source, target) in enumerate(zip(source_refs, targets))
    ]
    for fetch in fetches:
        fetch.start()
    dk_ref[...] = jnp.zeros_like(dk_ref)
    dv_ref[...] = jnp.zeros_like(dv_ref)
    for fetch in fetches[:9]:
        fetch.wait()
    for c in range(KVH):
        empty = kv_ref[:, (2 * c + 1) * HD : (2 * c + 1) * HD + 1].astype(F32) > 0.5 * EMPTY
        bias_ref[c] = jnp.broadcast_to(jnp.where(empty, NEG, 0.0), (keys, HD))
        kt_ref[c] = kv_ref[:, 2 * c * HD : (2 * c + 1) * HD].T
    fetches[9].wait()

    def key_head(h):
        return int(h >= HALF) if isinstance(h, int) else (h >= HALF).astype(jnp.int32)

    def scores(h, part, top):
        c = key_head(h)
        x = contract_last(kv_ref[part, columns(2 * c)], qg_ref[:, columns(h)])
        for u in chunks:
            here = slice(part.start + u, part.start + u + CHUNK)
            biased = x[u : u + CHUNK] + jnp.concatenate([bias_ref[c, here, :]] * (rows // HD), axis=1)
            x_ref[here, :] = biased
            top = jnp.maximum(top, jnp.max(fold(biased), axis=0))
        return top

    def weights(h, part, top, total, cross):
        dp = contract_last(kv_ref[part, columns(2 * key_head(h) + 1)], qg_ref[:, columns(QH + h)])
        for u in chunks:
            here = slice(part.start + u, part.start + u + CHUNK)
            e = jnp.exp2((x_ref[here, :] - top) * unit)
            y_ref[here, :] = e
            p_ref[here, :] = dp[u : u + CHUNK]
            total = total + jnp.sum(fold(e), axis=0)
            cross = cross + jnp.sum(fold(e * dp[u : u + CHUNK]), axis=0)
        return total, cross

    def gradients(h, part, q, g, share, row_dot, dqt):
        c = key_head(h)
        p, ds = [], []
        for u in chunks:
            here = slice(part.start + u, part.start + u + CHUNK)
            attend = y_ref[here, :] * share
            p.append(attend.astype(BF))
            ds.append((attend * (p_ref[here, :] - row_dot)).astype(BF))
        ds = jnp.concatenate(ds, axis=0)
        dv_ref[c, part, :] += dot(jnp.concatenate(p, axis=0), g)
        dk_ref[c, part, :] += dot(ds, q)
        return dqt + dot(kt_ref[c, :, part], ds)

    def step(i, top, total, cross):
        known = not isinstance(i, int)
        has_gradients = known or i >= 0
        has_weights = known or 0 <= i + 1 < QH
        has_scores = known or i + 2 < QH
        top = jnp.max(top, axis=0, keepdims=True)
        if has_gradients:
            share = 1.0 / jnp.sum(total, axis=0, keepdims=True)
            row_dot = jnp.sum(cross, axis=0, keepdims=True) * share
            q, g = qg_ref[:, columns(i)], qg_ref[:, columns(QH + i)]
        dqt = jnp.zeros((HD, rows), F32)
        next_top, next_total, next_cross = low, zero, zero
        for part in parts:
            if has_gradients:
                dqt = gradients(i, part, q, g, share, row_dot, dqt)
            if has_weights:
                next_total, next_cross = weights(i + 1, part, top, next_total, next_cross)
            if has_scores:
                next_top = scores(i + 2, part, next_top)
        if has_gradients:
            dq_ref[:, columns(i)] = (dqt * scale).T.astype(BF)
        return next_top, next_total, next_cross

    state = step(-1, *step(-2, low, zero, zero))
    state = lax.fori_loop(0, QH - 2, lambda i, state: step(i, *state), state)
    step(QH - 1, *step(QH - 2, *state))

    for i in range(8):
        here = slice(i * block, (i + 1) * block)
        for c in range(KVH):
            ref, first = (dkv_refs[i], 2 * c * HD) if i < 7 else (dkv_refs[7 + c], 0)
            ref[:, first : first + HD] = (dk_ref[c, here, :] * scale).astype(BF)
            ref[:, first + HD : first + 2 * HD] = dv_ref[c, here, :].astype(BF)


def unpack_q_kernel(head_ref, group_ref, dq_ref, out_ref, taker_ref):
    taker = taker_of(group_ref, dq_ref.shape[0])
    taker_ref[...] = taker
    for slot in range(QH):
        place = place_of(head_ref[slot])
        out_ref[:, slot * HD : (slot + 1) * HD] = dot(taker, dq_ref[:, columns(place)]).astype(BF)


def unpack_kv_kernel(taker_ref, dkv_ref, dk_ref, dv_ref):
    rows = dot(taker_ref[...], dkv_ref[...]).astype(BF)
    for c in range(KVH):
        cols = slice(c * HD, (c + 1) * HD)
        dk_ref[:, cols] = rows[:, 2 * c * HD : (2 * c + 1) * HD]
        dv_ref[:, cols] = rows[:, (2 * c + 1) * HD : (2 * c + 2) * HD]


def step_by(axis, distance):
    size = lax.axis_size(axis)
    pairs = [(i, (i + distance) % size) for i in range(size)]
    return lambda x: lax.ppermute(x, axis, pairs)


def gather_column(block):
    up, down = step_by(COLUMN, 1), step_by(COLUMN, -1)
    half = block.shape[1] // 2
    below = above = block
    blocks = [block]
    for i in range(3):
        if i == 2:
            far = [
                step_by(COLUMN, 2)(below[:, :half]),
                step_by(COLUMN, -2)(above[:, half:]),
            ]
        below, above = up(below), down(above)
        blocks += [below, above]
    return blocks + far


def scatter_column(blocks):
    up, down = step_by(COLUMN, 1), step_by(COLUMN, -1)

    def plus(*terms):
        return sum(term.astype(F32) for term in terms).astype(BF)

    own, to_below, to_above = blocks[0], blocks[1:7:2], blocks[2:7:2]
    zeros = jnp.zeros_like(blocks[7])
    far_up = jnp.concatenate([step_by(COLUMN, 2)(blocks[7]), zeros], axis=1)
    far_down = jnp.concatenate([zeros, step_by(COLUMN, -2)(blocks[8])], axis=1)
    rising = plus(to_above[1], up(to_above[2]), far_up)
    falling = plus(to_below[1], down(to_below[2]), far_down)
    rising, falling = plus(to_above[0], up(rising)), plus(to_below[0], down(falling))
    return plus(own, up(rising), down(falling))


def struct(*shape):
    return jax.ShapeDtypeStruct(shape, BF)


def call(kernel, name, out_shape, scalars=0, inputs=1, far=0, scratch=(), vmem=16, cost=None):
    whole = pl.BlockSpec(memory_space=pltpu.VMEM)
    many = isinstance(out_shape, tuple)
    return pl.pallas_call(
        kernel,
        out_shape=out_shape,
        in_specs=[pl.BlockSpec(memory_space=pltpu.SMEM)] * scalars
        + [whole] * inputs
        + [pl.BlockSpec(memory_space=pltpu.HBM)] * far,
        out_specs=(whole,) * len(out_shape) if many else whole,
        scratch_shapes=scratch,
        compiler_params=pltpu.CompilerParams(vmem_limit_bytes=vmem * MIB),
        cost_estimate=cost,
        name=name,
    )


def per_device(queries, keys, values, grad_out, group_of_row, head_slot):
    rows = queries.shape[0]
    groups = lax.axis_size(PLANE)
    column = lax.axis_size(COLUMN)
    slots = groups * CAP
    width_q = QH * HD
    width_kv = 2 * KVH * HD
    all_keys = column * slots
    row_group = group_of_row.reshape(1, rows)

    def over_plane(array):
        return lax.all_to_all(array, PLANE, split_axis=0, concat_axis=0, tiled=True)

    sent_kv = call(pack_kv_kernel, "pack_kv", struct(slots, width_kv), inputs=3, vmem=60)(row_group, keys, values)
    home_kv = over_plane(sent_kv)
    all_kv = gather_column(home_kv)
    sent_qg = call(
        pack_qg_kernel, "pack_qg", struct(slots, 2 * width_q), scalars=1, inputs=3, vmem=60
    )(
        head_slot, row_group, queries, grad_out
    )
    home_qg = over_plane(sent_qg)

    pairs = QH * slots * all_keys
    blocks = [struct(*block.shape) for block in all_kv]
    *grad_kv, grad_q = call(
        attend_kernel,
        "attend",
        (*blocks, struct(slots, width_q)),
        inputs=0,
        far=10,
        vmem=40,
        scratch=[
            pltpu.VMEM((slots, 2 * width_q), BF),
            pltpu.VMEM((all_keys, width_kv), BF),
            pltpu.VMEM((all_keys, slots), F32),
            pltpu.VMEM((all_keys, slots), F32),
            pltpu.VMEM((all_keys, slots), F32),
            pltpu.VMEM((KVH, all_keys, HD), F32),
            pltpu.VMEM((KVH, all_keys, HD), F32),
            pltpu.VMEM((KVH, all_keys, HD), F32),
            pltpu.VMEM((KVH, HD, all_keys), BF),
            pltpu.SemaphoreType.DMA((10,)),
        ],
        cost=pl.CostEstimate(
            flops=10 * HD * pairs,
            bytes_accessed=2 * (3 * slots * width_q + 2 * all_keys * width_kv),
            transcendentals=pairs,
        ),
    )(*all_kv, home_qg)

    kv_total = scatter_column(grad_kv)
    back_q = over_plane(grad_q)
    back_kv = over_plane(kv_total)
    out_q, taker = call(
        unpack_q_kernel, "unpack_q", (struct(rows, width_q), struct(rows, slots)), scalars=1, inputs=2
    )(head_slot, row_group, back_q)
    out_k, out_v = call(
        unpack_kv_kernel, "unpack_kv", (struct(rows, KVH * HD), struct(rows, KVH * HD)), inputs=2
    )(taker, back_kv)
    return out_q, out_k, out_v


def solution(mesh):
    fine = Mesh(mesh.devices.reshape(4, 4, 2, 2, 4), AXES)
    split = P(AXES, None)
    return jax.shard_map(
        per_device,
        mesh=fine,
        in_specs=(split, split, split, split, split, P()),
        out_specs=(split, split, split),
        check_vma=False,
    )
```

```python
import math

import jax
import jax.numpy as jnp
from jax import lax
from jax.experimental import pallas as pl
from jax.experimental.pallas import tpu as pltpu
from jax.sharding import Mesh
from jax.sharding import PartitionSpec as P

HD = 128
QH = 16
KVH = 2
GROUP_HEADS = 7
CAP = 8
HALF = QH // KVH
EMPTY = 64.0
NEG = -1e30
AXES = ("zh", "y", "c", "zl", "x")
PLANE = ("y", "c", "x")
COLUMN = ("zh", "zl")
BF = jnp.bfloat16
F32 = jnp.float32
KEY_TILE = 2048
CHUNK = 64
MIB = 1024 * 1024


def contract_last(left, right):
    return lax.dot_general(left, right, (((1,), (1,)), ((), ())), preferred_element_type=F32)


def dot(left, right):
    return jnp.dot(left, right, preferred_element_type=F32)


def columns(at, width=HD):
    return pl.ds(pl.multiple_of(at * width, width), width)


def place_of(head):
    real = head < KVH * GROUP_HEADS
    return jnp.where(
        real,
        head + (head >= GROUP_HEADS).astype(jnp.int32),
        (head - KVH * GROUP_HEADS) * HALF + GROUP_HEADS,
    )


def row_groups(group_ref):
    rows = group_ref.shape[1]
    along = jnp.broadcast_to(group_ref[...].astype(F32), (rows, rows))
    across = along.T
    first = lax.broadcasted_iota(jnp.int32, (rows, rows), 0)
    second = lax.broadcasted_iota(jnp.int32, (rows, rows), 1)
    return along, across, along == across, first < second


def placer_of(group_ref, slots):
    rows = group_ref.shape[1]
    along, across, same, earlier = row_groups(group_ref)
    before = jnp.sum(jnp.where(same & earlier, 1.0, 0.0), axis=0, keepdims=True)
    target = (along[:1] * CAP + before).astype(jnp.int32)
    return jnp.where(lax.broadcasted_iota(jnp.int32, (slots, rows), 0) == target, 1.0, 0.0).astype(BF)


def taker_of(group_ref, slots):
    rows = group_ref.shape[1]
    along, across, same, earlier = row_groups(group_ref)
    later = lax.broadcasted_iota(jnp.int32, (rows, rows), 0) > lax.broadcasted_iota(
        jnp.int32, (rows, rows), 1
    )
    before = jnp.sum(jnp.where(same & later, 1.0, 0.0), axis=1, keepdims=True)
    target = (across[:, :1] * CAP + before).astype(jnp.int32)
    return jnp.where(lax.broadcasted_iota(jnp.int32, (rows, slots), 1) == target, 1.0, 0.0).astype(BF)


def pack_kv_kernel(group_ref, key_ref, value_ref, out_ref):
    slots = out_ref.shape[0]
    placer = placer_of(group_ref, slots)
    filled = jnp.sum(placer.astype(F32), axis=1, keepdims=True)
    lane = lax.broadcasted_iota(jnp.int32, (slots, HD), 1)
    mark = jnp.where((lane == 0) & (filled < 0.5), EMPTY, 0.0)
    for c in range(KVH):
        cols = slice(c * HD, (c + 1) * HD)
        out_ref[:, 2 * c * HD : (2 * c + 1) * HD] = dot(placer, key_ref[:, cols]).astype(BF)
        out_ref[:, (2 * c + 1) * HD : (2 * c + 2) * HD] = (dot(placer, value_ref[:, cols]) + mark).astype(BF)


def pack_qg_kernel(head_ref, group_ref, query_ref, grad_ref, out_ref):
    placer = placer_of(group_ref, out_ref.shape[0])
    for slot in range(QH):
        cols = slice(slot * HD, (slot + 1) * HD)
        head = head_ref[slot]
        place = place_of(head)
        real = (head < KVH * GROUP_HEADS).astype(F32)
        out_ref[:, columns(place)] = dot(placer, query_ref[:, cols]).astype(BF)
        out_ref[:, columns(QH + place)] = (dot(placer, grad_ref[:, cols]) * real).astype(BF)


def attend_kernel(*refs):
    source_refs, dkv_refs, dq_ref = refs[:10], refs[10:19], refs[19]
    qg_ref, kv_ref, x_ref, y_ref, p_ref, dk_ref, dv_ref, bias_ref, kt_ref, sems = refs[20:]
    keys = kv_ref.shape[0]
    rows = qg_ref.shape[0]
    block = keys // 8
    scale = HD ** (-0.5)
    unit = scale * math.log2(math.e)
    parts = [slice(t, t + KEY_TILE) for t in range(0, keys, KEY_TILE)]
    chunks = range(0, KEY_TILE, CHUNK)
    low = jnp.full((8, rows), -3e38, F32)
    zero = jnp.zeros((8, rows), F32)

    def fold(tile):
        return tile.reshape(tile.shape[0] // 8, 8, rows)

    targets = [kv_ref.at[i * block : (i + 1) * block, :] for i in range(7)]
    targets += [kv_ref.at[7 * block :, : 2 * HD], kv_ref.at[7 * block :, 2 * HD :], qg_ref]
    fetches = [
        pltpu.make_async_copy(source, target, sems.at[i])
        for i, (source, target) in enumerate(zip(source_refs, targets))
    ]
    for fetch in fetches:
        fetch.start()
    dk_ref[...] = jnp.zeros_like(dk_ref)
    dv_ref[...] = jnp.zeros_like(dv_ref)
    for fetch in fetches[:9]:
        fetch.wait()
    for c in range(KVH):
        empty = kv_ref[:, (2 * c + 1) * HD : (2 * c + 1) * HD + 1].astype(F32) > 0.5 * EMPTY
        bias_ref[c] = jnp.broadcast_to(jnp.where(empty, NEG, 0.0), (keys, HD))
        kt_ref[c] = kv_ref[:, 2 * c * HD : (2 * c + 1) * HD].T
    fetches[9].wait()

    def key_head(h):
        return int(h >= HALF) if isinstance(h, int) else (h >= HALF).astype(jnp.int32)

    def scores(h, part, top):
        c = key_head(h)
        x = contract_last(kv_ref[part, columns(2 * c)], qg_ref[:, columns(h)])
        for u in chunks:
            here = slice(part.start + u, part.start + u + CHUNK)
            biased = x[u : u + CHUNK] + jnp.concatenate([bias_ref[c, here, :]] * (rows // HD), axis=1)
            x_ref[here, :] = biased
            top = jnp.maximum(top, jnp.max(fold(biased), axis=0))
        return top

    def weights(h, part, top, total, cross):
        dp = contract_last(kv_ref[part, columns(2 * key_head(h) + 1)], qg_ref[:, columns(QH + h)])
        for u in chunks:
            here = slice(part.start + u, part.start + u + CHUNK)
            e = jnp.exp2((x_ref[here, :] - top) * unit)
            y_ref[here, :] = e
            p_ref[here, :] = dp[u : u + CHUNK]
            total = total + jnp.sum(fold(e), axis=0)
            cross = cross + jnp.sum(fold(e * dp[u : u + CHUNK]), axis=0)
        return total, cross

    def gradients(h, part, q, g, share, row_dot, dqt):
        c = key_head(h)
        p, ds = [], []
        for u in chunks:
            here = slice(part.start + u, part.start + u + CHUNK)
            attend = y_ref[here, :] * share
            p.append(attend.astype(BF))
            ds.append((attend * (p_ref[here, :] - row_dot)).astype(BF))
        ds = jnp.concatenate(ds, axis=0)
        dv_ref[c, part, :] += dot(jnp.concatenate(p, axis=0), g)
        dk_ref[c, part, :] += dot(ds, q)
        return dqt + dot(kt_ref[c, :, part], ds)

    def step(i, top, total, cross):
        known = not isinstance(i, int)
        has_gradients = known or i >= 0
        has_weights = known or 0 <= i + 1 < QH
        has_scores = known or i + 2 < QH
        top = jnp.max(top, axis=0, keepdims=True)
        if has_gradients:
            share = 1.0 / jnp.sum(total, axis=0, keepdims=True)
            row_dot = jnp.sum(cross, axis=0, keepdims=True) * share
            q, g = qg_ref[:, columns(i)], qg_ref[:, columns(QH + i)]
        dqt = jnp.zeros((HD, rows), F32)
        next_top, next_total, next_cross = low, zero, zero
        for part in parts:
            if has_gradients:
                dqt = gradients(i, part, q, g, share, row_dot, dqt)
            if has_weights:
                next_total, next_cross = weights(i + 1, part, top, next_total, next_cross)
            if has_scores:
                next_top = scores(i + 2, part, next_top)
        if has_gradients:
            dq_ref[:, columns(i)] = (dqt * scale).T.astype(BF)
        return next_top, next_total, next_cross

    state = step(-1, *step(-2, low, zero, zero))
    state = lax.fori_loop(0, QH - 2, lambda i, state: step(i, *state), state)
    step(QH - 1, *step(QH - 2, *state))

    for i in range(8):
        here = slice(i * block, (i + 1) * block)
        for c in range(KVH):
            ref, first = (dkv_refs[i], 2 * c * HD) if i < 7 else (dkv_refs[7 + c], 0)
            ref[:, first : first + HD] = (dk_ref[c, here, :] * scale).astype(BF)
            ref[:, first + HD : first + 2 * HD] = dv_ref[c, here, :].astype(BF)


def unpack_q_kernel(head_ref, group_ref, dq_ref, out_ref, taker_ref):
    taker = taker_of(group_ref, dq_ref.shape[0])
    taker_ref[...] = taker
    for slot in range(QH):
        place = place_of(head_ref[slot])
        out_ref[:, slot * HD : (slot + 1) * HD] = dot(taker, dq_ref[:, columns(place)]).astype(BF)


def unpack_kv_kernel(taker_ref, dkv_ref, dk_ref, dv_ref):
    rows = dot(taker_ref[...], dkv_ref[...]).astype(BF)
    for c in range(KVH):
        cols = slice(c * HD, (c + 1) * HD)
        dk_ref[:, cols] = rows[:, 2 * c * HD : (2 * c + 1) * HD]
        dv_ref[:, cols] = rows[:, (2 * c + 1) * HD : (2 * c + 2) * HD]


def step_by(axis, distance):
    size = lax.axis_size(axis)
    pairs = [(i, (i + distance) % size) for i in range(size)]
    return lambda x: lax.ppermute(x, axis, pairs)


def gather_column(block):
    up, down = step_by(COLUMN, 1), step_by(COLUMN, -1)
    half = block.shape[1] // 2
    below = above = block
    blocks = [block]
    for i in range(3):
        if i == 2:
            far = [
                step_by(COLUMN, 2)(below[:, :half]),
                step_by(COLUMN, -2)(above[:, half:]),
            ]
        below, above = up(below), down(above)
        blocks += [below, above]
    return blocks + far


def scatter_column(blocks):
    up, down = step_by(COLUMN, 1), step_by(COLUMN, -1)

    def plus(*terms):
        return sum(term.astype(F32) for term in terms).astype(BF)

    own, to_below, to_above = blocks[0], blocks[1:7:2], blocks[2:7:2]
    zeros = jnp.zeros_like(blocks[7])
    far_up = jnp.concatenate([step_by(COLUMN, 2)(blocks[7]), zeros], axis=1)
    far_down = jnp.concatenate([zeros, step_by(COLUMN, -2)(blocks[8])], axis=1)
    rising = plus(to_above[1], up(to_above[2]), far_up)
    falling = plus(to_below[1], down(to_below[2]), far_down)
    rising, falling = plus(to_above[0], up(rising)), plus(to_below[0], down(falling))
    return plus(own, up(rising), down(falling))


def struct(*shape):
    return jax.ShapeDtypeStruct(shape, BF)


def call(kernel, name, out_shape, scalars=0, inputs=1, far=0, scratch=(), vmem=16, cost=None):
    whole = pl.BlockSpec(memory_space=pltpu.VMEM)
    many = isinstance(out_shape, tuple)
    return pl.pallas_call(
        kernel,
        out_shape=out_shape,
        in_specs=[pl.BlockSpec(memory_space=pltpu.SMEM)] * scalars
        + [whole] * inputs
        + [pl.BlockSpec(memory_space=pltpu.HBM)] * far,
        out_specs=(whole,) * len(out_shape) if many else whole,
        scratch_shapes=scratch,
        compiler_params=pltpu.CompilerParams(vmem_limit_bytes=vmem * MIB),
        cost_estimate=cost,
        name=name,
    )


def per_device(queries, keys, values, grad_out, group_of_row, head_slot):
    rows = queries.shape[0]
    groups = lax.axis_size(PLANE)
    column = lax.axis_size(COLUMN)
    slots = groups * CAP
    width_q = QH * HD
    width_kv = 2 * KVH * HD
    all_keys = column * slots
    row_group = group_of_row.reshape(1, rows)

    def over_plane(array):
        return lax.all_to_all(array, PLANE, split_axis=0, concat_axis=0, tiled=True)

    sent_kv = call(pack_kv_kernel, "pack_kv", struct(slots, width_kv), inputs=3, vmem=60)(row_group, keys, values)
    home_kv = over_plane(sent_kv)
    all_kv = gather_column(home_kv)
    sent_qg = call(
        pack_qg_kernel, "pack_qg", struct(slots, 2 * width_q), scalars=1, inputs=3, vmem=60
    )(
        head_slot, row_group, queries, grad_out
    )
    home_qg = over_plane(sent_qg)

    pairs = QH * slots * all_keys
    blocks = [struct(*block.shape) for block in all_kv]
    *grad_kv, grad_q = call(
        attend_kernel,
        "attend",
        (*blocks, struct(slots, width_q)),
        inputs=0,
        far=10,
        vmem=60,
        scratch=[
            pltpu.VMEM((slots, 2 * width_q), BF),
            pltpu.VMEM((all_keys, width_kv), BF),
            pltpu.VMEM((all_keys, slots), F32),
            pltpu.VMEM((all_keys, slots), F32),
            pltpu.VMEM((all_keys, slots), F32),
            pltpu.VMEM((KVH, all_keys, HD), F32),
            pltpu.VMEM((KVH, all_keys, HD), F32),
            pltpu.VMEM((KVH, all_keys, HD), F32),
            pltpu.VMEM((KVH, HD, all_keys), BF),
            pltpu.SemaphoreType.DMA((10,)),
        ],
        cost=pl.CostEstimate(
            flops=10 * HD * pairs,
            bytes_accessed=2 * (3 * slots * width_q + 2 * all_keys * width_kv),
            transcendentals=pairs,
        ),
    )(*all_kv, home_qg)

    kv_total = scatter_column(grad_kv)
    back_q = over_plane(grad_q)
    back_kv = over_plane(kv_total)
    out_q, taker = call(
        unpack_q_kernel, "unpack_q", (struct(rows, width_q), struct(rows, slots)), scalars=1, inputs=2
    )(head_slot, row_group, back_q)
    out_k, out_v = call(
        unpack_kv_kernel, "unpack_kv", (struct(rows, KVH * HD), struct(rows, KVH * HD)), inputs=2
    )(taker, back_kv)
    return out_q, out_k, out_v


def solution(mesh):
    fine = Mesh(mesh.devices.reshape(4, 4, 2, 2, 4), AXES)
    split = P(AXES, None)
    return jax.shard_map(
        per_device,
        mesh=fine,
        in_specs=(split, split, split, split, split, P()),
        out_specs=(split, split, split),
        check_vma=False,
    )
```

```python
import math

import jax
import jax.numpy as jnp
from jax import lax
from jax.experimental import pallas as pl
from jax.experimental.pallas import tpu as pltpu
from jax.sharding import Mesh
from jax.sharding import PartitionSpec as P

HD = 128
QH = 16
KVH = 2
GROUP_HEADS = 7
CAP = 8
HALF = QH // KVH
EMPTY = 64.0
NEG = -1e30
AXES = ("zh", "y", "c", "zl", "x")
PLANE = ("y", "c", "x")
COLUMN = ("zh", "zl")
BF = jnp.bfloat16
F32 = jnp.float32
KEY_TILE = 2048
CHUNK = 64
MIB = 1024 * 1024


def contract_last(left, right):
    return lax.dot_general(left, right, (((1,), (1,)), ((), ())), preferred_element_type=F32)


def dot(left, right):
    return jnp.dot(left, right, preferred_element_type=F32)


def columns(at, width=HD):
    return pl.ds(pl.multiple_of(at * width, width), width)


def place_of(head):
    real = head < KVH * GROUP_HEADS
    return jnp.where(
        real,
        head + (head >= GROUP_HEADS).astype(jnp.int32),
        (head - KVH * GROUP_HEADS) * HALF + GROUP_HEADS,
    )


def row_groups(group_ref):
    rows = group_ref.shape[1]
    along = jnp.broadcast_to(group_ref[...].astype(F32), (rows, rows))
    across = along.T
    first = lax.broadcasted_iota(jnp.int32, (rows, rows), 0)
    second = lax.broadcasted_iota(jnp.int32, (rows, rows), 1)
    return along, across, along == across, first < second


def placer_of(group_ref, slots):
    rows = group_ref.shape[1]
    along, across, same, earlier = row_groups(group_ref)
    before = jnp.sum(jnp.where(same & earlier, 1.0, 0.0), axis=0, keepdims=True)
    target = (along[:1] * CAP + before).astype(jnp.int32)
    return jnp.where(lax.broadcasted_iota(jnp.int32, (slots, rows), 0) == target, 1.0, 0.0).astype(BF)


def taker_of(group_ref, slots):
    rows = group_ref.shape[1]
    along, across, same, earlier = row_groups(group_ref)
    later = lax.broadcasted_iota(jnp.int32, (rows, rows), 0) > lax.broadcasted_iota(
        jnp.int32, (rows, rows), 1
    )
    before = jnp.sum(jnp.where(same & later, 1.0, 0.0), axis=1, keepdims=True)
    target = (across[:, :1] * CAP + before).astype(jnp.int32)
    return jnp.where(lax.broadcasted_iota(jnp.int32, (rows, slots), 1) == target, 1.0, 0.0).astype(BF)


def pack_kv_kernel(group_ref, key_ref, value_ref, out_ref):
    slots = out_ref.shape[0]
    placer = placer_of(group_ref, slots)
    filled = jnp.sum(placer.astype(F32), axis=1, keepdims=True)
    lane = lax.broadcasted_iota(jnp.int32, (slots, HD), 1)
    mark = jnp.where((lane == 0) & (filled < 0.5), EMPTY, 0.0)
    for c in range(KVH):
        cols = slice(c * HD, (c + 1) * HD)
        out_ref[:, 2 * c * HD : (2 * c + 1) * HD] = dot(placer, key_ref[:, cols]).astype(BF)
        out_ref[:, (2 * c + 1) * HD : (2 * c + 2) * HD] = (dot(placer, value_ref[:, cols]) + mark).astype(BF)


def pack_qg_kernel(head_ref, group_ref, query_ref, grad_ref, out_ref):
    placer = placer_of(group_ref, out_ref.shape[0])
    for slot in range(QH):
        cols = slice(slot * HD, (slot + 1) * HD)
        head = head_ref[slot]
        place = place_of(head)
        real = (head < KVH * GROUP_HEADS).astype(F32)
        out_ref[:, columns(place)] = dot(placer, query_ref[:, cols]).astype(BF)
        out_ref[:, columns(QH + place)] = (dot(placer, grad_ref[:, cols]) * real).astype(BF)


def attend_kernel(*refs):
    source_refs, dkv_refs, dq_ref = refs[:10], refs[10:19], refs[19]
    qg_ref, kv_ref, x_ref, y_ref, p_ref, dk_ref, dv_ref, bias_ref, kt_ref, sems = refs[20:]
    keys = kv_ref.shape[0]
    rows = qg_ref.shape[0]
    block = keys // 8
    scale = HD ** (-0.5)
    unit = scale * math.log2(math.e)
    parts = [slice(t, t + KEY_TILE) for t in range(0, keys, KEY_TILE)]
    chunks = range(0, KEY_TILE, CHUNK)
    low = jnp.full((8, rows), -3e38, F32)
    zero = jnp.zeros((8, rows), F32)

    def fold(tile):
        return tile.reshape(tile.shape[0] // 8, 8, rows)

    targets = [kv_ref.at[i * block : (i + 1) * block, :] for i in range(7)]
    targets += [kv_ref.at[7 * block :, : 2 * HD], kv_ref.at[7 * block :, 2 * HD :], qg_ref]
    fetches = [
        pltpu.make_async_copy(source, target, sems.at[i])
        for i, (source, target) in enumerate(zip(source_refs, targets))
    ]
    for fetch in fetches:
        fetch.start()
    dk_ref[...] = jnp.zeros_like(dk_ref)
    dv_ref[...] = jnp.zeros_like(dv_ref)
    for fetch in fetches[:9]:
        fetch.wait()
    for c in range(KVH):
        empty = kv_ref[:, (2 * c + 1) * HD : (2 * c + 1) * HD + 1].astype(F32) > 0.5 * EMPTY
        bias_ref[c] = jnp.broadcast_to(jnp.where(empty, NEG, 0.0), (keys, HD))
        kt_ref[c] = kv_ref[:, 2 * c * HD : (2 * c + 1) * HD].T
    fetches[9].wait()

    def key_head(h):
        return int(h >= HALF) if isinstance(h, int) else (h >= HALF).astype(jnp.int32)

    def scores(h, part, top):
        c = key_head(h)
        x = contract_last(kv_ref[part, columns(2 * c)], qg_ref[:, columns(h)])
        for u in chunks:
            here = slice(part.start + u, part.start + u + CHUNK)
            biased = x[u : u + CHUNK] + jnp.concatenate([bias_ref[c, here, :]] * (rows // HD), axis=1)
            x_ref[here, :] = biased
            top = jnp.maximum(top, jnp.max(fold(biased), axis=0))
        return top

    def weights(h, part, top, total, cross):
        dp = contract_last(kv_ref[part, columns(2 * key_head(h) + 1)], qg_ref[:, columns(QH + h)])
        for u in chunks:
            here = slice(part.start + u, part.start + u + CHUNK)
            e = jnp.exp2((x_ref[here, :] - top) * unit)
            y_ref[here, :] = e
            p_ref[here, :] = dp[u : u + CHUNK]
            total = total + jnp.sum(fold(e), axis=0)
            cross = cross + jnp.sum(fold(e * dp[u : u + CHUNK]), axis=0)
        return total, cross

    def gradients(h, part, q, g, share, row_dot, dqt):
        c = key_head(h)
        p, ds = [], []
        for u in chunks:
            here = slice(part.start + u, part.start + u + CHUNK)
            attend = y_ref[here, :] * share
            p.append(attend.astype(BF))
            ds.append((attend * (p_ref[here, :] - row_dot)).astype(BF))
        ds = jnp.concatenate(ds, axis=0)
        dv_ref[c, part, :] += dot(jnp.concatenate(p, axis=0), g)
        dk_ref[c, part, :] += dot(ds, q)
        return dqt + dot(kt_ref[c, :, part], ds)

    def step(i, top, total, cross):
        known = not isinstance(i, int)
        has_gradients = known or i >= 0
        has_weights = known or 0 <= i + 1 < QH
        has_scores = known or i + 2 < QH
        top = jnp.max(top, axis=0, keepdims=True)
        if has_gradients:
            share = 1.0 / jnp.sum(total, axis=0, keepdims=True)
            row_dot = jnp.sum(cross, axis=0, keepdims=True) * share
            q, g = qg_ref[:, columns(i)], qg_ref[:, columns(QH + i)]
        dqt = jnp.zeros((HD, rows), F32)
        next_top, next_total, next_cross = low, zero, zero
        for part in parts:
            if has_gradients:
                dqt = gradients(i, part, q, g, share, row_dot, dqt)
            if has_weights:
                next_total, next_cross = weights(i + 1, part, top, next_total, next_cross)
            if has_scores:
                next_top = scores(i + 2, part, next_top)
        if has_gradients:
            dq_ref[:, columns(i)] = (dqt * scale).T.astype(BF)
        return next_top, next_total, next_cross

    state = step(-1, *step(-2, low, zero, zero))
    state = lax.fori_loop(0, QH - 2, lambda i, state: step(i, *state), state)
    step(QH - 1, *step(QH - 2, *state))

    for i in range(8):
        here = slice(i * block, (i + 1) * block)
        for c in range(KVH):
            ref, first = (dkv_refs[i], 2 * c * HD) if i < 7 else (dkv_refs[7 + c], 0)
            ref[:, first : first + HD] = (dk_ref[c, here, :] * scale).astype(BF)
            ref[:, first + HD : first + 2 * HD] = dv_ref[c, here, :].astype(BF)


def unpack_q_kernel(head_ref, group_ref, dq_ref, out_ref, taker_ref):
    taker = taker_of(group_ref, dq_ref.shape[0])
    taker_ref[...] = taker
    for slot in range(QH):
        place = place_of(head_ref[slot])
        out_ref[:, slot * HD : (slot + 1) * HD] = dot(taker, dq_ref[:, columns(place)]).astype(BF)


def unpack_kv_kernel(taker_ref, dkv_ref, dk_ref, dv_ref):
    rows = dot(taker_ref[...], dkv_ref[...]).astype(BF)
    for c in range(KVH):
        cols = slice(c * HD, (c + 1) * HD)
        dk_ref[:, cols] = rows[:, 2 * c * HD : (2 * c + 1) * HD]
        dv_ref[:, cols] = rows[:, (2 * c + 1) * HD : (2 * c + 2) * HD]


def step_by(axis, distance):
    size = lax.axis_size(axis)
    pairs = [(i, (i + distance) % size) for i in range(size)]
    return lambda x: lax.ppermute(x, axis, pairs)


def gather_column(block):
    up, down = step_by(COLUMN, 1), step_by(COLUMN, -1)
    half = block.shape[1] // 2
    below = above = block
    blocks = [block]
    for i in range(3):
        if i == 2:
            far = [
                step_by(COLUMN, 2)(below[:, :half]),
                step_by(COLUMN, -2)(above[:, half:]),
            ]
        below, above = up(below), down(above)
        blocks += [below, above]
    return blocks + far


def scatter_column(blocks):
    up, down = step_by(COLUMN, 1), step_by(COLUMN, -1)

    def plus(*terms):
        return sum(term.astype(F32) for term in terms).astype(BF)

    own, to_below, to_above = blocks[0], blocks[1:7:2], blocks[2:7:2]
    zeros = jnp.zeros_like(blocks[7])
    far_up = jnp.concatenate([step_by(COLUMN, 2)(blocks[7]), zeros], axis=1)
    far_down = jnp.concatenate([zeros, step_by(COLUMN, -2)(blocks[8])], axis=1)
    rising = plus(to_above[1], up(to_above[2]), far_up)
    falling = plus(to_below[1], down(to_below[2]), far_down)
    rising, falling = plus(to_above[0], up(rising)), plus(to_below[0], down(falling))
    return plus(own, up(rising), down(falling))


def struct(*shape):
    return jax.ShapeDtypeStruct(shape, BF)


def call(kernel, name, out_shape, scalars=0, inputs=1, far=0, scratch=(), vmem=16, cost=None):
    whole = pl.BlockSpec(memory_space=pltpu.VMEM)
    many = isinstance(out_shape, tuple)
    return pl.pallas_call(
        kernel,
        out_shape=out_shape,
        in_specs=[pl.BlockSpec(memory_space=pltpu.SMEM)] * scalars
        + [whole] * inputs
        + [pl.BlockSpec(memory_space=pltpu.HBM)] * far,
        out_specs=(whole,) * len(out_shape) if many else whole,
        scratch_shapes=scratch,
        compiler_params=pltpu.CompilerParams(vmem_limit_bytes=vmem * MIB),
        cost_estimate=cost,
        name=name,
    )


def per_device(queries, keys, values, grad_out, group_of_row, head_slot):
    rows = queries.shape[0]
    groups = lax.axis_size(PLANE)
    column = lax.axis_size(COLUMN)
    slots = groups * CAP
    width_q = QH * HD
    width_kv = 2 * KVH * HD
    all_keys = column * slots
    row_group = group_of_row.reshape(1, rows)

    def over_plane(array):
        return lax.all_to_all(array, PLANE, split_axis=0, concat_axis=0, tiled=True)

    sent_kv = call(pack_kv_kernel, "pack_kv", struct(slots, width_kv), inputs=3, vmem=60)(row_group, keys, values)
    home_kv = over_plane(sent_kv)
    all_kv = gather_column(home_kv)
    sent_qg = call(
        pack_qg_kernel, "pack_qg", struct(slots, 2 * width_q), scalars=1, inputs=3, vmem=60
    )(
        head_slot, row_group, queries, grad_out
    )
    home_qg = over_plane(sent_qg)

    pairs = QH * slots * all_keys
    blocks = [struct(*block.shape) for block in all_kv]
    *grad_kv, grad_q = call(
        attend_kernel,
        "attend",
        (*blocks, struct(slots, width_q)),
        inputs=0,
        far=10,
        vmem=57,
        scratch=[
            pltpu.VMEM((slots, 2 * width_q), BF),
            pltpu.VMEM((all_keys, width_kv), BF),
            pltpu.VMEM((all_keys, slots), F32),
            pltpu.VMEM((all_keys, slots), F32),
            pltpu.VMEM((all_keys, slots), F32),
            pltpu.VMEM((KVH, all_keys, HD), F32),
            pltpu.VMEM((KVH, all_keys, HD), F32),
            pltpu.VMEM((KVH, all_keys, HD), F32),
            pltpu.VMEM((KVH, HD, all_keys), BF),
            pltpu.SemaphoreType.DMA((10,)),
        ],
        cost=pl.CostEstimate(
            flops=10 * HD * pairs,
            bytes_accessed=2 * (3 * slots * width_q + 2 * all_keys * width_kv),
            transcendentals=pairs,
        ),
    )(*all_kv, home_qg)

    kv_total = scatter_column(grad_kv)
    back_q = over_plane(grad_q)
    back_kv = over_plane(kv_total)
    out_q, taker = call(
        unpack_q_kernel, "unpack_q", (struct(rows, width_q), struct(rows, slots)), scalars=1, inputs=2
    )(head_slot, row_group, back_q)
    out_k, out_v = call(
        unpack_kv_kernel, "unpack_kv", (struct(rows, KVH * HD), struct(rows, KVH * HD)), inputs=2
    )(taker, back_kv)
    return out_q, out_k, out_v


def solution(mesh):
    fine = Mesh(mesh.devices.reshape(4, 4, 2, 2, 4), AXES)
    split = P(AXES, None)
    return jax.shard_map(
        per_device,
        mesh=fine,
        in_specs=(split, split, split, split, split, P()),
        out_specs=(split, split, split),
        check_vma=False,
    )
```
